32 devices in a mesh: dp: 16 (over z, y, core), seq: 2 (over x).
Axes of the slice: x: 2, y: 2, z: 4, core: 2. Of those that a mesh axis runs over, the one named last changes fastest.
Arguments:
- images: bfloat16 [32, 256, 2048], P('dp', 'seq'), may hold values from -6 to 6
- captions: bfloat16 [32, 128, 4096], P('dp', 'seq'), may hold values from -6 to 6
- cap_lengths: int32 [32], P('dp'), may hold values from 5 to 128, as said below
- norm1_gain: bfloat16 [2048], P('dp'), may hold values from 0.25 to 1.75
- w_query: bfloat16 [2048, 2048], P('dp'), may hold values from -0.125 to 0.125
- w_key: bfloat16 [2048, 2048], P('dp'), may hold values from -0.125 to 0.125
- w_value: bfloat16 [2048, 2048], P('dp'), may hold values from -0.125 to 0.125
- w_out: bfloat16 [2048, 2048], P('dp'), may hold values from -0.5 to 0.5
- norm2_gain: bfloat16 [2048], P('dp'), may hold values from 0.25 to 1.75
- w_text: bfloat16 [4096, 2048], P('dp'), may hold values from -0.09375 to 0.09375
- w_cross_query: bfloat16 [2048, 2048], P('dp'), may hold values from -0.125 to 0.125
- w_cross_key: bfloat16 [2048, 2048], P('dp'), may hold values from -0.125 to 0.125
- w_cross_value: bfloat16 [2048, 2048], P('dp'), may hold values from -0.125 to 0.125
- w_cross_out: bfloat16 [2048, 2048], P('dp'), may hold values from -0.5 to 0.5
- norm3_gain: bfloat16 [2048], P('dp'), may hold values from 0.25 to 1.75
- w_up: bfloat16 [2048, 8192], P('dp'), may hold values from -0.125 to 0.125
- w_down: bfloat16 [8192, 2048], P('dp'), may hold values from -0.0625 to 0.0625
- out_grad: bfloat16 [32, 256, 2048], P('dp', 'seq'), may hold values from -6 to 6
Outputs:
- layer_out: bfloat16 [32, 256, 2048], P('dp', 'seq')
- image_grad: float32 [32, 256, 2048], P('dp', 'seq')
- caption_grad: float32 [32, 128, 4096], P('dp', 'seq')
- grad_norm1: float32 [2048], P('dp')
- grad_query: float32 [2048, 2048], P('dp')
- grad_key: float32 [2048, 2048], P('dp')
- grad_value: float32 [2048, 2048], P('dp')
- grad_out: float32 [2048, 2048], P('dp')
- grad_norm2: float32 [2048], P('dp')
- grad_text: float32 [4096, 2048], P('dp')
- grad_cross_query: float32 [2048, 2048], P('dp')
- grad_cross_key: float32 [2048, 2048], P('dp')
- grad_cross_value: float32 [2048, 2048], P('dp')
- grad_cross_out: float32 [2048, 2048], P('dp')
- grad_norm3: float32 [2048], P('dp')
- grad_up: float32 [2048, 8192], P('dp')
- grad_down: float32 [8192, 2048], P('dp')
The draws below stay inside these ranges and needn't reach their ends.
Inputs may be any that keep to these rules, and one draw needn't show every extreme that they name: `cap_lengths`: caption slots at and after a caption's length are padding. Of the 2 images of each index of dp, at least one has all 128 slots real.
All inputs are finite; a program needn't handle non-finite values.
Results may differ from the reference program's by a relative error of at most 0.024.
Values may be sent and summed in bfloat16 or wider, within the bound.
A program may use at most 640 MiB of HBM per device.

```python
import jax
import jax.numpy as jnp
from jax import lax

D = 2048
HEADS = 16
HEAD_DIM = 128
FF = 8192
TEXT_D = 4096
IMG_TOKENS = 256
CAPTION = 128
IMG_DEV = 2
IMAGES = 32


def draw_cap_lengths(key, part):
    key = jax.random.fold_in(key, 7)
    key_base, key_pick = jax.random.split(key)
    spread_len = jax.random.randint(key_base, (IMAGES,), 5, CAPTION + 1)
    chosen = jax.random.randint(key_pick, (IMAGES // IMG_DEV,), 0, IMG_DEV)
    slot_index = jnp.arange(IMAGES) % IMG_DEV
    full_row = slot_index == jnp.repeat(chosen, IMG_DEV)
    return jnp.where(full_row, CAPTION, spread_len).astype(jnp.int32)


def shard_levels(stream_key, extent, pieces, low, high):
    gain, own = 1.0, jax.random.fold_in(stream_key, 6)
    for dim, shards_of in pieces:
        steps = jnp.exp(jax.random.uniform(jax.random.fold_in(own, dim), (shards_of,), jnp.float32, low / len(pieces), high / len(pieces)))
        gain = gain * jnp.repeat(steps, extent[dim] // shards_of).reshape([-1 if axis == dim else 1 for axis in range(len(extent))])
    return gain


def noise(own_key, dims, width, bound, cuts=(), kind=jnp.bfloat16):
    factor_of = shard_levels(own_key, dims, cuts, -0.22, 0.18) if cuts else 1.0
    values = jax.random.normal(own_key, dims, jnp.float32) * width * factor_of
    return jnp.minimum(jnp.maximum(values, -bound), bound).astype(kind)


def setup_inputs(seed: int = 0) -> dict:
    arg_keys = jax.random.split(jax.random.key(seed), 19)
    images = noise(arg_keys[0], (IMAGES, IMG_TOKENS, D), 1.0, 6.0, ((0, 16), (1, 2)))
    captions = noise(arg_keys[1], (IMAGES, CAPTION, TEXT_D), 1.0, 6.0, ((0, 16), (1, 2)))
    cap_lengths = draw_cap_lengths(jax.random.fold_in(arg_keys[18], 71), 0)
    norm1_gain = jnp.clip(1.0 + 0.15 * jax.random.normal(arg_keys[3], (D,), jnp.float32), 0.25, 1.75).astype(jnp.bfloat16)
    w_query = noise(arg_keys[4], (D, D), D ** -0.5, 0.125, ((0, 16),))
    w_key = noise(arg_keys[5], (D, D), D ** -0.5, 0.125, ((0, 16),))
    w_value = noise(arg_keys[6], (D, D), D ** -0.5, 0.125, ((0, 16),))
    w_out = noise(arg_keys[7], (D, D), (D // 16) ** -0.5, 0.5, ((0, 16),))
    norm2_gain = jnp.clip(1.0 + 0.15 * jax.random.normal(arg_keys[8], (D,), jnp.float32), 0.25, 1.75).astype(jnp.bfloat16)
    w_text = noise(arg_keys[9], (TEXT_D, D), TEXT_D ** -0.5, 0.09375, ((0, 16),))
    w_cross_query = noise(arg_keys[10], (D, D), D ** -0.5, 0.125, ((0, 16),))
    w_cross_key = noise(arg_keys[11], (D, D), D ** -0.5, 0.125, ((0, 16),))
    w_cross_value = noise(arg_keys[12], (D, D), D ** -0.5, 0.125, ((0, 16),))
    w_cross_out = noise(arg_keys[13], (D, D), (D // 16) ** -0.5, 0.5, ((0, 16),))
    norm3_gain = jnp.clip(1.0 + 0.15 * jax.random.normal(arg_keys[14], (D,), jnp.float32), 0.25, 1.75).astype(jnp.bfloat16)
    w_up = noise(arg_keys[15], (D, FF), D ** -0.5, 0.125, ((0, 16),))
    w_down = noise(arg_keys[16], (FF, D), FF ** -0.5, 0.0625, ((0, 16),))
    out_grad = noise(arg_keys[17], (IMAGES, IMG_TOKENS, D), 1.0, 6.0, ((0, 16), (1, 2)))
    return {"images": images, "captions": captions, "cap_lengths": cap_lengths, "norm1_gain": norm1_gain, "w_query": w_query, "w_key": w_key, "w_value": w_value, "w_out": w_out, "norm2_gain": norm2_gain, "w_text": w_text, "w_cross_query": w_cross_query, "w_cross_key": w_cross_key, "w_cross_value": w_cross_value, "w_cross_out": w_cross_out, "norm3_gain": norm3_gain, "w_up": w_up, "w_down": w_down, "out_grad": out_grad}


EPSILON = 1e-05

@jax.custom_vjp
def low(v):
    return lax.optimization_barrier(v.astype(jnp.bfloat16)).astype(jnp.float32)

@jax.custom_vjp
def low_back(v):
    return v

def low_keep(v):
    return (low(v), None)

def low_pass(kept, grad):
    return (grad,)

def back_keep(v):
    return (v, None)

def back_low(kept, grad):
    return (low(grad),)
low.defvjp(low_keep, low_pass)
low_back.defvjp(back_keep, back_low)

def round_both(values):
    return low(low_back(values))

def product(form, left, right):
    return jnp.einsum(form, left, right, precision=lax.Precision.HIGHEST)

def layer_norm(values, norm_gain):
    centred = values - lax.optimization_barrier(jnp.mean(values, axis=-1, keepdims=True))
    spread = lax.optimization_barrier(jnp.mean(centred * centred, axis=-1, keepdims=True))
    return centred * lax.rsqrt(spread + EPSILON) * norm_gain

def split_heads(values):
    return values.reshape(values.shape[0], values.shape[1], HEADS, HEAD_DIM)

def attention(queries, key_rows, value_rows, usable):
    score_scale = HEAD_DIM ** (-0.5)
    raw_scores = low_back(product('bqhd,bkhd->bhqk', split_heads(queries), split_heads(key_rows)))
    scores = raw_scores * score_scale
    if usable is not None:
        scores = jnp.where(usable[:, None, None, :], scores, -1e+30)
    chances = low(jax.nn.softmax(scores, axis=-1))
    blended = product('bhqk,bkhd->bqhd', chances, split_heads(value_rows))
    return round_both(blended.reshape(queries.shape))

def layer(stream, text_rows, lengths, params):
    norm1_gain, w_query, w_key, w_value, w_out, norm2_gain, w_text, w_cross_query, w_cross_key, w_cross_value, w_cross_out, norm3_gain, w_up, w_down = params
    normed1 = low(layer_norm(stream, norm1_gain))
    queries = round_both(product('bsk,kn->bsn', normed1, w_query))
    key_rows = round_both(product('bsk,kn->bsn', normed1, w_key))
    value_rows = round_both(product('bsk,kn->bsn', normed1, w_value))
    self_mix = attention(queries, key_rows, value_rows, None)
    after_self = stream + low_back(product('bsk,kn->bsn', self_mix, w_out))
    normed2 = low(layer_norm(after_self, norm2_gain))
    caption_feat = round_both(product('bsk,kn->bsn', text_rows, w_text))
    cross_keys = round_both(product('bsk,kn->bsn', caption_feat, w_cross_key))
    cross_values = round_both(product('bsk,kn->bsn', caption_feat, w_cross_value))
    cross_queries = round_both(product('bsk,kn->bsn', normed2, w_cross_query))
    usable = jnp.arange(CAPTION)[None, :] < lengths[:, None]
    cross_mix = attention(cross_queries, cross_keys, cross_values, usable)
    after_cross = after_self + low_back(product('bsk,kn->bsn', cross_mix, w_cross_out))
    normed3 = low(layer_norm(after_cross, norm3_gain))
    hidden = low_back(product('bsk,kn->bsn', normed3, w_up))
    active = round_both(jax.nn.gelu(hidden, approximate=False))
    return after_cross + low_back(product('bsk,kn->bsn', active, w_down))

def reference(images, captions, cap_lengths, norm1_gain, w_query, w_key, w_value, w_out, norm2_gain, w_text, w_cross_query, w_cross_key, w_cross_value, w_cross_out, norm3_gain, w_up, w_down, out_grad):
    params = tuple((weight.astype(jnp.float32) for weight in (norm1_gain, w_query, w_key, w_value, w_out, norm2_gain, w_text, w_cross_query, w_cross_key, w_cross_value, w_cross_out, norm3_gain, w_up, w_down)))
    group = 16
    rounds = IMAGES // group
    stream_all = images.astype(jnp.float32).reshape(rounds, group, IMG_TOKENS, D)
    text_all = captions.astype(jnp.float32).reshape(rounds, group, CAPTION, TEXT_D)
    length_all = cap_lengths.astype(jnp.int32).reshape(rounds, group)
    cotangent_all = out_grad.astype(jnp.float32).reshape(rounds, group, IMG_TOKENS, D)

    def one_group(totals, inputs):
        stream, text_rows, lengths, cotangent = inputs

        def forward(stream_in, text_in, params_in):
            return layer(stream_in, text_in, lengths, params_in)
        result, pullback = jax.vjp(forward, stream, text_rows, params)
        grad_stream, grad_rows, grad_params = pullback(cotangent)
        totals = tuple((total + grad for total, grad in zip(totals, grad_params)))
        return (totals, (result, grad_stream, grad_rows))
    start_totals = tuple((jnp.zeros_like(weight) for weight in params))
    totals, (results, grad_streams, grad_texts) = lax.scan(one_group, start_totals, (stream_all, text_all, length_all, cotangent_all))
    layer_out = results.reshape(IMAGES, IMG_TOKENS, D).astype(jnp.bfloat16)
    image_grad = grad_streams.reshape(IMAGES, IMG_TOKENS, D)
    caption_grad = grad_texts.reshape(IMAGES, CAPTION, TEXT_D)
    return (layer_out, image_grad, caption_grad, totals[0], totals[1], totals[2], totals[3], totals[4], totals[5], totals[6], totals[7], totals[8], totals[9], totals[10], totals[11], totals[12], totals[13])
```

```python
import functools

import jax
import jax.numpy as jnp
from jax import lax
from jax.experimental import pallas as pl
from jax.experimental.pallas import tpu as pltpu
from jax.sharding import PartitionSpec as P

HEADS = 16
HEAD_DIM = 128
EPSILON = 1e-05
SCALE = HEAD_DIM ** (-0.5)
BF16 = jnp.bfloat16
F32 = jnp.float32
TP_HEADS = HEADS // 4
TP_WIDTH = TP_HEADS * HEAD_DIM


def rounded(values):
    return values.astype(BF16)


def mm(left, right):
    return lax.dot_general(left, right, (((1,), (0,)), ((), ())), preferred_element_type=F32)


def mm_t(left, right):
    return lax.dot_general(left, right, (((1,), (1,)), ((), ())), preferred_element_type=F32)


def outer(left, right):
    return lax.dot_general(left, right, (((0,), (0,)), ((), ())), preferred_element_type=F32)


def layer_norm(values, norm_gain):
    centred = values - jnp.mean(values, axis=-1, keepdims=True)
    spread = jnp.mean(centred * centred, axis=-1, keepdims=True)
    return centred * lax.rsqrt(spread + EPSILON) * norm_gain


def norm_back(values, norm_gain, grad_normed):
    centred = values - jnp.mean(values, axis=-1, keepdims=True)
    inverse = lax.rsqrt(jnp.mean(centred * centred, axis=-1, keepdims=True) + EPSILON)
    unit = centred * inverse
    scaled = grad_normed * norm_gain
    result = inverse * (
        scaled
        - jnp.mean(scaled, axis=-1, keepdims=True)
        - unit * jnp.mean(scaled * unit, axis=-1, keepdims=True)
    )
    return result, jnp.sum(grad_normed * unit, axis=tuple(range(values.ndim - 1)))


def exact_gelu(values):
    return jax.nn.gelu(values, approximate=False)


def dot_nt(left, right):
    return lax.dot_general(left, right, (((1,), (1,)), ((), ())), preferred_element_type=F32)


def dot_nn(left, right):
    return lax.dot_general(left, right, (((1,), (0,)), ((), ())), preferred_element_type=F32)


def dot_tn(left, right):
    return lax.dot_general(left, right, (((0,), (0,)), ((), ())), preferred_element_type=F32)


def soft(queries, keys, usable):
    scores = dot_nt(queries, keys) * SCALE
    if usable is not None:
        scores = jnp.where(usable, scores, -1e30)
    grown = jnp.exp(scores - jnp.max(scores, axis=-1, keepdims=True))
    return grown / jnp.sum(grown, axis=-1, keepdims=True)


def cut(ref, index):
    return ref[0, :, index * HEAD_DIM : (index + 1) * HEAD_DIM]


def put(ref, index, values):
    ref[0, :, index * HEAD_DIM : (index + 1) * HEAD_DIM] = values.astype(ref.dtype)


def attend_body(query_ref, query_at, pair_ref, key_at, value_at, usable, mix_ref):
    for head in range(TP_HEADS):
        prob = soft(cut(query_ref, query_at + head), cut(pair_ref, key_at + head), usable)
        put(mix_ref, head, dot_nn(rounded(prob), cut(pair_ref, value_at + head)))


def attend_back_body(
    query_ref, query_at, pair_ref, key_at, value_at, usable, grad_ref, gquery_ref, gpair_ref
):
    for head in range(TP_HEADS):
        queries = cut(query_ref, query_at + head)
        keys = cut(pair_ref, key_at + head)
        values = cut(pair_ref, value_at + head)
        grad_mix = cut(grad_ref, head)
        prob = soft(queries, keys, usable)
        grad_prob = dot_nt(grad_mix, values)
        put(gpair_ref, value_at + head, dot_tn(rounded(prob), grad_mix))
        grad_scores = prob * (grad_prob - jnp.sum(prob * grad_prob, axis=-1, keepdims=True))
        grad_raw = rounded(grad_scores * SCALE)
        put(gquery_ref, query_at + head, dot_nn(grad_raw, keys))
        put(gpair_ref, key_at + head, dot_tn(grad_raw, queries))


def self_kernel(qkv_ref, mix_ref):
    attend_body(qkv_ref, 0, qkv_ref, TP_HEADS, 2 * TP_HEADS, None, mix_ref)


def self_back_kernel(qkv_ref, grad_ref, gqkv_ref):
    attend_back_body(
        qkv_ref, 0, qkv_ref, TP_HEADS, 2 * TP_HEADS, None, grad_ref, gqkv_ref, gqkv_ref
    )


def cross_kernel(query_ref, pair_ref, usable_ref, mix_ref):
    attend_body(query_ref, 0, pair_ref, 0, TP_HEADS, usable_ref[0] > 0, mix_ref)


def cross_back_kernel(query_ref, pair_ref, usable_ref, grad_ref, gquery_ref, gpair_ref):
    attend_back_body(
        query_ref, 0, pair_ref, 0, TP_HEADS, usable_ref[0] > 0, grad_ref, gquery_ref, gpair_ref
    )


def per_image(kernel, outs, *args):
    images = args[0].shape[0]

    def block(shape):
        return pl.BlockSpec((1,) + tuple(shape[1:]), lambda i: (i, 0, 0))

    many = [jax.ShapeDtypeStruct(shape, BF16) for shape in outs]
    return pl.pallas_call(
        kernel,
        grid=(images,),
        in_specs=[block(arg.shape) for arg in args],
        out_specs=[block(shape) for shape in outs],
        out_shape=many,
        compiler_params=pltpu.CompilerParams(vmem_limit_bytes=32 * 1024 * 1024),
    )(*args)


def make(devices):
    planes = 4
    spread = devices // (2 * planes)
    half_spread = spread // 2
    groups = [
        [(a * 2 + y) * spread + b for a in range(planes) for b in range(spread)] for y in range(2)
    ]

    def swap(values, over_y, over_x):
        if not over_y:
            return lax.ppermute(values, "seq", [(0, 1), (1, 0)])
        if not over_x:
            return lax.ppermute(values, "dp", [(d, d ^ spread) for d in range(devices)])
        pairs = [(2 * d + x, 2 * (d ^ spread) + 1 - x) for d in range(devices) for x in range(2)]
        return lax.ppermute(values, ("dp", "seq"), pairs)

    def shuffle(values):
        lead = values.shape[:-1]
        blocks = values.reshape(lead + (planes, 2, spread, -1))
        return jnp.swapaxes(blocks, -3, -2).reshape(values.shape)

    def unshuffle(values):
        lead = values.shape[:-1]
        blocks = values.reshape(lead + (planes, spread, 2, -1))
        return jnp.swapaxes(blocks, -3, -2).reshape(values.shape)

    def gather_tokens(own):
        over_x, over_y, over_both = swap(own, 0, 1), swap(own, 1, 0), swap(own, 1, 1)
        near = jnp.stack([own, over_x], axis=1)
        far = jnp.stack([over_y, over_both], axis=1)
        images, tokens, features = own.shape
        return jnp.stack([near, far]).reshape(2 * images, 2 * tokens, features)

    def scatter_tokens(parts):
        images, tokens, features = parts.shape
        parts = parts.reshape(2, images // 2, 2, tokens // 2, features)
        total = parts[0, :, 0].astype(F32) + swap(parts[0, :, 1], 0, 1).astype(F32)
        total = total + swap(parts[1, :, 0], 1, 0).astype(F32)
        return total + swap(parts[1, :, 1], 1, 1).astype(F32)

    def gather_weight(payload):
        return lax.all_gather(payload, "dp", axis=0, tiled=True, axis_index_groups=groups)

    def reduce_weight(parts):
        return lax.psum_scatter(
            parts, "dp", scatter_dimension=0, tiled=True, axis_index_groups=groups
        )

    def on_device(
        images,
        captions,
        cap_lengths,
        norm1_gain,
        w_query,
        w_key,
        w_value,
        w_out,
        norm2_gain,
        w_text,
        w_cross_query,
        w_cross_key,
        w_cross_value,
        w_cross_out,
        norm3_gain,
        w_up,
        w_down,
        out_grad,
    ):
        d = lax.axis_index("dp")
        x = lax.axis_index("seq")
        y = (d // spread) % 2
        top = (d % spread) // half_spread
        d_model = images.shape[-1]
        ff_rows = w_down.shape[0]
        ff = ff_rows * devices
        group_images, group_tokens = 2 * images.shape[0], 2 * images.shape[1]
        slots = 2 * captions.shape[1]


        def head_columns(weight, yy):
            first = (2 * yy + x) * HEAD_DIM
            return [
                lax.dynamic_slice_in_dim(weight, 4 * HEAD_DIM * a + first, HEAD_DIM, 1)
                for a in range(planes)
            ]

        def heads_of(weights, yy):
            return jnp.concatenate([c for w in weights for c in head_columns(w, yy)], axis=1)

        def up_columns(yy):
            return jnp.concatenate(
                [
                    lax.dynamic_slice_in_dim(
                        w_up,
                        ((a * 2 + yy) * spread + b) * ff_rows + x * (ff_rows // 2),
                        ff_rows // 2,
                        1,
                    )
                    for a in range(planes)
                    for b in range(spread)
                ],
                axis=1,
            )

        def text_columns(yy):
            return lax.dynamic_slice_in_dim(w_text, (2 * yy + x) * TP_WIDTH, TP_WIDTH, 1)

        def both_rows(columns):
            own, other = columns(y), swap(columns(1 - y), 1, 0)
            first = jnp.where(y == 0, own, other)
            second = jnp.where(y == 0, other, own)
            return jnp.concatenate([first, second], axis=0)

        def pass_top(values):
            return lax.ppermute(values, "dp", [(i, i ^ half_spread) for i in range(devices)])

        def head_rows(weight):
            half = weight.shape[0] // 2
            kept = lax.dynamic_slice_in_dim(weight, top * half, half, 0)
            passed = lax.dynamic_slice_in_dim(weight, (1 - top) * half, half, 0)
            payload = jnp.where(top == x, kept, pass_top(passed))
            full = gather_weight(payload).reshape(planes, 2, half_spread, half, -1)
            return jnp.swapaxes(full, 1, 2).reshape(TP_WIDTH, -1)

        image_all = gather_tokens(shuffle(images))
        qkv_full = gather_weight(
            both_rows(lambda yy: heads_of((w_query, w_key, w_value), yy))
        )
        gains = lax.all_gather(
            jnp.stack([norm1_gain, norm2_gain, norm3_gain]), "dp", axis=1, tiled=True
        ).astype(F32)
        out_full = head_rows(w_out)
        caption_all = gather_tokens(shuffle(captions)).reshape(group_images * slots, -1)
        text_full = gather_weight(both_rows(text_columns))
        cross_full = gather_weight(
            both_rows(lambda yy: heads_of((w_cross_query, w_cross_key, w_cross_value), yy))
        )
        cquery_full, cpair_full = cross_full[:, :TP_WIDTH], cross_full[:, TP_WIDTH:]
        cout_full = head_rows(w_cross_out)
        up_full = gather_weight(both_rows(up_columns))
        down_full = gather_weight(
            lax.dynamic_slice_in_dim(w_down, x * (ff_rows // 2), ff_rows // 2, 0)
        )
        out_grad_all = gather_tokens(out_grad).reshape(-1, d_model)

        all_lengths = jnp.concatenate([cap_lengths, swap(cap_lengths, 1, 0)])
        position = jnp.arange(slots // 2)
        place = jnp.concatenate([x * (slots // 2) + position, (1 - x) * (slots // 2) + position])
        usable = (place[None, :] < all_lengths[:, None]).astype(F32)[:, None, :]

        stream = images.astype(F32)
        normed1 = rounded(layer_norm(image_all.astype(F32), shuffle(gains[0])))
        normed1 = normed1.reshape(-1, d_model)
        qkv = rounded(mm(normed1, qkv_full)).reshape(group_images, group_tokens, -1)
        (self_mix,) = per_image(
            self_kernel, [(group_images, group_tokens, TP_WIDTH)], qkv
        )
        self_mix = self_mix.reshape(-1, TP_WIDTH)
        self_part = rounded(mm(self_mix, out_full)).reshape(group_images, group_tokens, d_model)
        after_self = stream + scatter_tokens(self_part)

        quarter = 2 * y + x
        part_feat = rounded(mm(caption_all, text_full))

        def inner_shuffle(values, back):
            outer_dim, inner_dim = (spread, 2) if back else (2, spread)
            blocks = values.reshape(values.shape[0], outer_dim, inner_dim, -1)
            return jnp.swapaxes(blocks, 1, 2).reshape(values.shape)

        def swap_slots(values, ky, kx):
            rows = swap(values, ky, kx).reshape(2, group_images // 2, 2, slots // 2, -1)
            rows = rows[::-1] if ky else rows
            rows = rows[:, :, ::-1] if kx else rows
            return rows.reshape(values.shape)

        part_feat = inner_shuffle(part_feat, False)
        caption_feat = jnp.zeros((group_images * slots, d_model), BF16)
        for ky in range(2):
            for kx in range(2):
                piece = swap_slots(part_feat, ky, kx) if ky or kx else part_feat
                caption_feat = lax.dynamic_update_slice(
                    caption_feat, piece, (0, (quarter ^ (2 * ky + kx)) * TP_WIDTH)
                )
        cpair = rounded(mm(caption_feat, cpair_full)).reshape(group_images, slots, -1)

        normed2 = rounded(layer_norm(after_self, gains[1]))
        normed2 = gather_tokens(shuffle(normed2)).reshape(-1, d_model)
        cquery = rounded(mm(normed2, cquery_full)).reshape(group_images, group_tokens, -1)
        (cross_mix,) = per_image(
            cross_kernel, [(group_images, group_tokens, TP_WIDTH)], cquery, cpair, usable
        )
        cross_mix = cross_mix.reshape(-1, TP_WIDTH)
        cross_part = rounded(mm(cross_mix, cout_full)).reshape(group_images, group_tokens, d_model)
        after_cross = after_self + scatter_tokens(cross_part)

        normed3 = rounded(layer_norm(after_cross, gains[2]))
        normed3 = gather_tokens(shuffle(normed3)).reshape(-1, d_model)
        hidden = mm(normed3, up_full)
        active = rounded(exact_gelu(hidden))
        grad_down_part = rounded(outer(active, out_grad_all))
        layer_part = rounded(mm(active, down_full)).reshape(group_images, group_tokens, d_model)
        layer_out = rounded(after_cross + scatter_tokens(layer_part))

        grad_active = rounded(mm_t(out_grad_all, down_full))
        gelu_value, gelu_pull = jax.vjp(exact_gelu, hidden)
        grad_hidden = rounded(gelu_pull(grad_active.astype(F32))[0])
        grad_normed3 = rounded(mm_t(grad_hidden, up_full))
        grad_up_part = rounded(outer(normed3, grad_hidden))
        grad_normed3 = unshuffle(
            scatter_tokens(grad_normed3.reshape(group_images, group_tokens, d_model))
        )
        grad_stream, grad_norm3 = norm_back(after_cross, gains[2], grad_normed3)
        grad_after_cross = out_grad.astype(F32) + grad_stream

        branch2 = gather_tokens(rounded(grad_after_cross)).reshape(-1, d_model)
        grad_cross_mix = rounded(mm_t(branch2, cout_full))
        grad_cout_part = rounded(outer(cross_mix, branch2))
        gcquery, gcpair = per_image(
            cross_back_kernel,
            [cquery.shape, cpair.shape],
            cquery,
            cpair,
            usable,
            grad_cross_mix.reshape(group_images, group_tokens, TP_WIDTH),
        )
        gcquery = gcquery.reshape(-1, TP_WIDTH)
        gcpair = gcpair.reshape(-1, 2 * TP_WIDTH)
        grad_normed2 = rounded(mm_t(gcquery, cquery_full))
        grad_normed2 = unshuffle(
            scatter_tokens(grad_normed2.reshape(group_images, group_tokens, d_model))
        )
        grad_cross_part = rounded(
            jnp.concatenate([outer(normed2, gcquery), outer(caption_feat, gcpair)], axis=1)
        )
        grad_stream, grad_norm2 = norm_back(after_self, gains[1], grad_normed2)
        grad_after_self = grad_after_cross + grad_stream

        grad_feat_part = rounded(mm_t(gcpair, cpair_full))
        grad_feat = None
        for ky in range(2):
            for kx in range(2):
                piece = lax.dynamic_slice_in_dim(
                    grad_feat_part, (quarter ^ (2 * ky + kx)) * TP_WIDTH, TP_WIDTH, 1
                )
                if ky or kx:
                    grad_feat = grad_feat + swap_slots(piece, ky, kx).astype(F32)
                else:
                    grad_feat = piece.astype(F32)
        grad_feat = inner_shuffle(rounded(grad_feat), True)
        grad_text_part = rounded(outer(caption_all, grad_feat))
        caption_part = rounded(mm_t(grad_feat, text_full)).reshape(group_images, slots, -1)
        caption_grad = unshuffle(scatter_tokens(caption_part))

        branch1 = gather_tokens(rounded(grad_after_self)).reshape(-1, d_model)
        grad_self_mix = rounded(mm_t(branch1, out_full))
        (gqkv,) = per_image(
            self_back_kernel,
            [qkv.shape],
            qkv,
            grad_self_mix.reshape(group_images, group_tokens, TP_WIDTH),
        )
        gqkv = gqkv.reshape(-1, 3 * TP_WIDTH)
        grad_qkv_part = rounded(outer(normed1, gqkv))
        grad_out_part = rounded(outer(self_mix, branch1))
        grad_normed1 = rounded(mm_t(gqkv, qkv_full))
        grad_normed1 = unshuffle(
            scatter_tokens(grad_normed1.reshape(group_images, group_tokens, d_model))
        )
        grad_stream, grad_norm1 = norm_back(stream, gains[0], grad_normed1)
        image_grad = grad_after_self + grad_stream


        def rows_back(parts):
            summed = reduce_weight(parts)
            rows = summed.shape[0] // 2
            own = jnp.where(y == 0, summed[:rows], summed[rows:])
            other = jnp.where(y == 0, summed[rows:], summed[:rows])
            near = [own, swap(own, 0, 1)]
            far = [swap(other, 1, 0), swap(other, 1, 1)]
            near = [jnp.where(x == 0, near[0], near[1]), jnp.where(x == 0, near[1], near[0])]
            far = [jnp.where(x == 0, far[0], far[1]), jnp.where(x == 0, far[1], far[0])]
            return [
                [jnp.where(y == 0, near[i], far[i]) for i in range(2)],
                [jnp.where(y == 0, far[i], near[i]) for i in range(2)],
            ]

        def heads_back(pieces, at):
            return jnp.concatenate(
                [
                    pieces[yy][xx][:, at + a * HEAD_DIM : at + (a + 1) * HEAD_DIM]
                    for a in range(planes)
                    for yy in range(2)
                    for xx in range(2)
                ],
                axis=1,
            ).astype(F32)

        def head_rows_back(parts):
            columns = parts.shape[1]
            rows = TP_WIDTH // (planes * spread)
            parts = parts.reshape(planes, half_spread, 2, rows, columns)
            own = reduce_weight(jnp.swapaxes(parts, 1, 2).reshape(TP_WIDTH, columns))
            other = pass_top(own)
            whole = jnp.concatenate(
                [jnp.where(top == 0, own, other), jnp.where(top == 0, other, own)], axis=0
            )
            return jnp.where(top == x, whole, swap(whole, 0, 1)).astype(F32)

        half_down = reduce_weight(grad_down_part)
        other_down = swap(half_down, 0, 1)
        grad_down = jnp.concatenate(
            [
                jnp.where(x == 0, half_down, other_down),
                jnp.where(x == 0, other_down, half_down),
            ],
            axis=0,
        ).astype(F32)

        up_pieces = rows_back(grad_up_part)
        step = ff_rows // 2
        grad_up = jnp.concatenate(
            [
                up_pieces[yy][xx][:, (a * spread + b) * step : (a * spread + b + 1) * step]
                for a in range(planes)
                for yy in range(2)
                for b in range(spread)
                for xx in range(2)
            ],
            axis=1,
        ).astype(F32)
        grad_cross_out = head_rows_back(grad_cout_part)
        cross_pieces = rows_back(grad_cross_part)
        text_pieces = rows_back(grad_text_part)
        grad_text = jnp.concatenate(
            [text_pieces[yy][xx] for yy in range(2) for xx in range(2)], axis=1
        ).astype(F32)
        grad_out = head_rows_back(grad_out_part)
        qkv_pieces = rows_back(grad_qkv_part)

        norm_sums = lax.psum(
            jnp.stack([grad_norm1, grad_norm2, grad_norm3]), ("dp", "seq")
        )
        norm_rows = norm1_gain.shape[0]
        norm_sums = lax.dynamic_slice_in_dim(norm_sums, d * norm_rows, norm_rows, 1)
        return (
            layer_out,
            image_grad,
            caption_grad,
            norm_sums[0],
            heads_back(qkv_pieces, 0),
            heads_back(qkv_pieces, TP_WIDTH),
            heads_back(qkv_pieces, 2 * TP_WIDTH),
            grad_out,
            norm_sums[1],
            grad_text,
            heads_back(cross_pieces, 0),
            heads_back(cross_pieces, TP_WIDTH),
            heads_back(cross_pieces, 2 * TP_WIDTH),
            grad_cross_out,
            norm_sums[2],
            grad_up,
            grad_down,
        )

    return on_device


def solution(mesh):
    tokens = P("dp", "seq", None)
    rows = P("dp", None)
    vector = P("dp")
    in_specs = (
        (tokens, tokens, vector)
        + (vector, rows, rows, rows, rows)
        + (vector, rows, rows, rows, rows, rows)
        + (vector, rows, rows)
        + (tokens,)
    )
    out_specs = (
        (tokens, tokens, tokens)
        + (vector, rows, rows, rows, rows)
        + (vector, rows, rows, rows, rows, rows)
        + (vector, rows, rows)
    )
    return jax.shard_map(
        make(mesh.shape["dp"]), mesh=mesh, in_specs=in_specs, out_specs=out_specs, check_vma=False
    )
```

```python
import functools

import jax
import jax.numpy as jnp
from jax import lax
from jax.experimental import pallas as pl
from jax.experimental.pallas import tpu as pltpu
from jax.sharding import PartitionSpec as P

HEADS = 16
HEAD_DIM = 128
EPSILON = 1e-05
SCALE = HEAD_DIM ** (-0.5)
BF16 = jnp.bfloat16
F32 = jnp.float32
TP_HEADS = HEADS // 4
TP_WIDTH = TP_HEADS * HEAD_DIM


def rounded(values):
    return values.astype(BF16)


def after(values, *earlier):
    return lax.optimization_barrier((values,) + earlier)[0]


def after_all(pieces, *earlier):
    return list(after(tuple(pieces), *earlier))


def mm(left, right):
    return lax.dot_general(left, right, (((1,), (0,)), ((), ())), preferred_element_type=F32)


def mm_t(left, right):
    return lax.dot_general(left, right, (((1,), (1,)), ((), ())), preferred_element_type=F32)


def outer(left, right):
    return lax.dot_general(left, right, (((0,), (0,)), ((), ())), preferred_element_type=F32)


def layer_norm(values, norm_gain):
    centred = values - jnp.mean(values, axis=-1, keepdims=True)
    spread = jnp.mean(centred * centred, axis=-1, keepdims=True)
    return centred * lax.rsqrt(spread + EPSILON) * norm_gain


def norm_back(values, norm_gain, grad_normed):
    centred = values - jnp.mean(values, axis=-1, keepdims=True)
    inverse = lax.rsqrt(jnp.mean(centred * centred, axis=-1, keepdims=True) + EPSILON)
    unit = centred * inverse
    scaled = grad_normed * norm_gain
    result = inverse * (
        scaled
        - jnp.mean(scaled, axis=-1, keepdims=True)
        - unit * jnp.mean(scaled * unit, axis=-1, keepdims=True)
    )
    return result, jnp.sum(grad_normed * unit, axis=tuple(range(values.ndim - 1)))


def feed_forward_kernel(*refs):
    normed_refs, grad_refs = refs[:4], refs[4:8]
    up, down, active_ref, grad_hidden_ref, normed, out_grad = refs[8:]
    rows = normed_refs[0].shape[0]

    @pl.when(pl.program_id(0) == 0)
    def _():
        for k in range(4):
            normed[k * rows : (k + 1) * rows, :] = normed_refs[k][...]
            out_grad[k * rows : (k + 1) * rows, :] = grad_refs[k][...]

    for part in range(2):
        here = slice(2 * part * rows, 2 * (part + 1) * rows)
        hidden = mm(normed[here, :], up[...])
        half = 0.5 * (1.0 + lax.erf(hidden * (0.5**0.5)))
        active_ref[here, :] = rounded(hidden * half)
        grad_active = rounded(mm_t(out_grad[here, :], down[...])).astype(F32)
        slope = half + hidden * (jnp.exp(-0.5 * hidden * hidden) * (0.5 / jnp.pi) ** 0.5)
        grad_hidden_ref[here, :] = rounded(slope * grad_active)


def feed_forward(normed, out_grad, up, down, block=256):
    rows, d_model = normed[0].shape
    hidden = up.shape[1]
    whole = pl.BlockSpec((rows, d_model), lambda i: (0, 0), pipeline_mode=pl.Buffered(1))
    result = jax.ShapeDtypeStruct((4 * rows, hidden), BF16)
    return pl.pallas_call(
        feed_forward_kernel,
        grid=(hidden // block,),
        in_specs=[whole] * 8
        + [
            pl.BlockSpec((d_model, block), lambda i: (0, i)),
            pl.BlockSpec((block, d_model), lambda i: (i, 0)),
        ],
        out_specs=[pl.BlockSpec((4 * rows, block), lambda i: (0, i))] * 2
        + [pl.BlockSpec((4 * rows, d_model), lambda i: (0, 0))] * 2,
        out_shape=[result, result] + [jax.ShapeDtypeStruct((4 * rows, d_model), BF16)] * 2,
        compiler_params=pltpu.CompilerParams(vmem_limit_bytes=56 * 1024 * 1024),
    )(*normed, *out_grad, up, down)


def soft(queries, keys, usable):
    scores = mm_t(queries, keys) * SCALE
    if usable is not None:
        scores = jnp.where(usable, scores, -1e30)
    grown = jnp.exp(scores - jnp.max(scores, axis=-1, keepdims=True))
    return grown / jnp.sum(grown, axis=-1, keepdims=True)


def columns_at(index):
    return slice(index * HEAD_DIM, (index + 1) * HEAD_DIM)


def cut(refs, ky, index):
    return jnp.concatenate([refs[2 * ky + kx][0, :, columns_at(index)] for kx in range(2)], axis=0)


def put(refs, ky, index, values):
    rows = values.shape[0] // 2
    for kx in range(2):
        part = values[kx * rows : (kx + 1) * rows]
        refs[2 * ky + kx][0, :, columns_at(index)] = part.astype(BF16)


def attend_body(queries, pairs, key_at, value_at, usable, mix):
    for ky in range(2):
        for head in range(TP_HEADS):
            mask = None if usable is None else usable[ky, 0] > 0
            prob = soft(cut(queries, ky, head), cut(pairs, ky, key_at + head), mask)
            put(mix, ky, head, mm(rounded(prob), cut(pairs, ky, value_at + head)))


def attend_back_body(queries, pairs, key_at, value_at, usable, grads, gqueries, gpairs):
    for ky in range(2):
        for head in range(TP_HEADS):
            mask = None if usable is None else usable[ky, 0] > 0
            query_rows = cut(queries, ky, head)
            key_rows = cut(pairs, ky, key_at + head)
            grad_mix = cut(grads, ky, head)
            prob = soft(query_rows, key_rows, mask)
            grad_prob = mm_t(grad_mix, cut(pairs, ky, value_at + head))
            put(gpairs, ky, value_at + head, outer(rounded(prob), grad_mix))
            grad_scores = prob * (grad_prob - jnp.sum(prob * grad_prob, axis=-1, keepdims=True))
            grad_raw = rounded(grad_scores * SCALE)
            put(gqueries, ky, head, mm(grad_raw, key_rows))
            put(gpairs, ky, key_at + head, outer(grad_raw, query_rows))


def self_kernel(*refs):
    attend_body(refs[:4], refs[:4], TP_HEADS, 2 * TP_HEADS, None, refs[4:])


def self_back_kernel(*refs):
    attend_back_body(
        refs[:4], refs[:4], TP_HEADS, 2 * TP_HEADS, None, refs[4:8], refs[8:], refs[8:]
    )


def cross_kernel(usable, *refs):
    attend_body(refs[:4], refs[4:8], 0, TP_HEADS, usable, refs[8:])


def cross_back_kernel(usable, *refs):
    attend_back_body(
        refs[:4], refs[4:8], 0, TP_HEADS, usable, refs[8:12], refs[12:16], refs[16:]
    )


def per_image(kernel, usable, pieces, widths):
    images = pieces[0].shape[0]

    def block(shape):
        return pl.BlockSpec((1,) + tuple(shape[1:]), lambda i: (i, 0, 0))

    shapes = [
        pieces[like].shape[:2] + (width,) for like, width in widths for _ in range(4)
    ]
    in_specs = [block(piece.shape) for piece in pieces]
    if usable is not None:
        slots = usable.shape[-1]
        in_specs = [pl.BlockSpec((2, 1, 1, slots), lambda i: (0, i, 0, 0))] + in_specs
        pieces = [usable] + list(pieces)
    return pl.pallas_call(
        kernel,
        grid=(images,),
        in_specs=in_specs,
        out_specs=[block(shape) for shape in shapes],
        out_shape=[jax.ShapeDtypeStruct(shape, BF16) for shape in shapes],
        compiler_params=pltpu.CompilerParams(vmem_limit_bytes=48 * 1024 * 1024),
    )(*pieces)


def whole_call(kernel, place, args, shapes, dtype=BF16):
    vmem = pl.BlockSpec(memory_space=pltpu.VMEM)
    return pl.pallas_call(
        kernel,
        in_specs=[pl.BlockSpec(memory_space=pltpu.SMEM)] + [vmem] * len(args),
        out_specs=[vmem] * len(shapes),
        out_shape=[jax.ShapeDtypeStruct(shape, dtype) for shape in shapes],
        compiler_params=pltpu.CompilerParams(vmem_limit_bytes=48 * 1024 * 1024),
    )(place, *args)


def joined(refs):
    return jnp.concatenate([ref[...] for ref in refs], axis=0)


def put_head_rows(target, column, mix, grads):
    full = outer(joined(mix), joined(grads))
    half = full.shape[0] // 2
    kept = jnp.where(pl.program_id(0) % 2 == 0, full[:half], full[half:]).astype(BF16)
    for j in range(4):
        target[j * half : (j + 1) * half, column:] = kept[:, j * TP_WIDTH : (j + 1) * TP_WIDTH]


def self_weights_kernel(*refs):
    normed, branch, gqkv, mix, target = refs[:4], refs[4:8], refs[8:12], refs[12:16], refs[16]
    wide = 3 * TP_WIDTH
    target[:, :wide] = outer(joined(normed), joined(gqkv)).astype(BF16)
    put_head_rows(target, wide, mix, branch)


def cross_weights_kernel(*refs):
    normed, branch, gquery, mix = refs[:4], refs[4:8], refs[8:12], refs[12:16]
    feat, gpair, target = refs[16:]
    wide = TP_WIDTH
    target[:, :wide] = outer(joined(normed), joined(gquery)).astype(BF16)
    target[:, wide : 3 * wide] = outer(feat[...], gpair[...]).astype(BF16)
    put_head_rows(target, 3 * wide, mix, branch)


def text_weights_kernel(*refs):
    low, high, gfeat, target = refs[:4], refs[4:8], refs[8], refs[9]
    target[:, :TP_WIDTH] = outer(joined(low), gfeat[...]).astype(BF16)
    target[:, TP_WIDTH:] = outer(joined(high), gfeat[...]).astype(BF16)


def weight_call(kernel, d_model, columns, args, specs, blocks):
    rows = d_model // blocks
    return pl.pallas_call(
        kernel,
        grid=(blocks,),
        in_specs=specs,
        out_specs=pl.BlockSpec((rows, columns), lambda i: (i, 0)),
        out_shape=jax.ShapeDtypeStruct((d_model, columns), BF16),
        compiler_params=pltpu.CompilerParams(vmem_limit_bytes=56 * 1024 * 1024),
    )(*args)


def column_block(rows, columns, index):
    return pl.BlockSpec((rows, columns), lambda i: (0, index(i)))


def whole_block(array):
    return pl.BlockSpec(array.shape, lambda i: (0, 0), pipeline_mode=pl.Buffered(1))


def self_weights(normed, branch, gqkv, mix, blocks=8):
    tokens, d_model = normed[0].shape
    rows = d_model // blocks
    specs = [column_block(tokens, rows, lambda i: i)] * 4
    specs += [whole_block(a) for a in branch + gqkv]
    specs += [column_block(tokens, HEAD_DIM, lambda i: i // 2)] * 4
    args = (*normed, *branch, *gqkv, *mix)
    return weight_call(self_weights_kernel, d_model, 4 * TP_WIDTH, args, specs, blocks)


def cross_weights(normed, branch, feat, gquery, gpair, mix, blocks=8):
    tokens, d_model = normed[0].shape
    rows = d_model // blocks
    specs = [column_block(tokens, rows, lambda i: i)] * 4
    specs += [whole_block(a) for a in branch + gquery]
    specs += [column_block(tokens, HEAD_DIM, lambda i: i // 2)] * 4
    specs += [column_block(feat.shape[0], rows, lambda i: i), whole_block(gpair)]
    args = (*normed, *branch, *gquery, *mix, feat, gpair)
    return weight_call(cross_weights_kernel, d_model, 4 * TP_WIDTH, args, specs, blocks)


def text_weights(captions, gfeat, blocks=8):
    slots, text_d = captions[0].shape
    rows = text_d // 2 // blocks
    specs = [column_block(slots, rows, lambda i: i)] * 4
    specs += [column_block(slots, rows, lambda i: i + blocks)] * 4 + [whole_block(gfeat)]
    args = (*captions, *captions, gfeat)
    return weight_call(text_weights_kernel, text_d // 2, 2 * TP_WIDTH, args, specs, blocks)


def make(devices, planes=4):
    spread = devices // (2 * planes)
    half_spread = spread // 2
    groups = [
        [(a * 2 + y) * spread + b for a in range(planes) for b in range(spread)] for y in range(2)
    ]

    def swap(values, over_y, over_x):
        if not over_y:
            return lax.ppermute(values, "seq", [(0, 1), (1, 0)])
        if not over_x:
            return lax.ppermute(values, "dp", [(d, d ^ spread) for d in range(devices)])
        pairs = [(2 * d + x, 2 * (d ^ spread) + 1 - x) for d in range(devices) for x in range(2)]
        return lax.ppermute(values, ("dp", "seq"), pairs)

    def flip(values, bit):
        return lax.ppermute(values, "dp", [(d, d ^ bit) for d in range(devices)])

    def shuffle(values):
        lead = values.shape[:-1]
        blocks = values.reshape(lead + (planes, 2, spread, -1))
        return jnp.swapaxes(blocks, -3, -2).reshape(values.shape)

    def unshuffle(values):
        lead = values.shape[:-1]
        blocks = values.reshape(lead + (planes, spread, 2, -1))
        return jnp.swapaxes(blocks, -3, -2).reshape(values.shape)

    def gather_tokens(own):
        half = own.shape[0] // 2
        over_x, over_y = swap(own, 0, 1), swap(own, 1, 0)
        far = jnp.concatenate([swap(over_y[:half], 0, 1), swap(over_x[half:], 1, 0)], axis=0)
        return [own, over_x, over_y, far]

    def gather_direct(own):
        return [own, swap(own, 0, 1), swap(own, 1, 0), swap(own, 1, 1)]

    def scatter_tokens(parts):
        here, to_x, to_y, far = lax.optimization_barrier(tuple(parts))
        half = here.shape[0] // 2
        by_x, by_y = swap(far[:half], 0, 1), swap(far[half:], 1, 0)
        to_y = jnp.concatenate([rounded(to_y[:half].astype(F32) + by_x), to_y[half:]], axis=0)
        to_x = jnp.concatenate([to_x[:half], rounded(to_x[half:].astype(F32) + by_y)], axis=0)
        total = here.astype(F32) + swap(to_x, 0, 1).astype(F32)
        return total + swap(to_y, 1, 0).astype(F32), (to_x, to_y)

    def gather_weight(payload):
        return lax.all_gather(payload, "dp", axis=0, tiled=True, axis_index_groups=groups)

    def reduce_weight(parts):
        return lax.psum_scatter(
            parts, "dp", scatter_dimension=0, tiled=True, axis_index_groups=groups
        )

    def gather_small(values, d):
        bit = 1
        while bit < devices:
            other = flip(values, bit)
            low = (d & bit) == 0
            values = jnp.concatenate(
                [jnp.where(low, values, other), jnp.where(low, other, values)], axis=1
            )
            bit *= 2
        return values

    def reduce_small(values, d):
        values = values + swap(values, 0, 1)
        bit = devices // 2
        while bit:
            half = values.shape[1] // 2
            low = (d & bit) == 0
            kept = jnp.where(low, values[:, :half], values[:, half:])
            values = kept + flip(jnp.where(low, values[:, half:], values[:, :half]), bit)
            bit //= 2
        return values


    def copy_heads(place, weights, own, other, at):
        y, x = place[0], place[1]
        for yy, target in ((y, own), (1 - y, other)):
            for index, weight in enumerate(weights):
                for a in range(planes):
                    start = pl.multiple_of((4 * a + 2 * yy + x) * HEAD_DIM, HEAD_DIM)
                    column = at + index * TP_WIDTH + a * HEAD_DIM
                    target[:, column : column + HEAD_DIM] = weight[:, pl.ds(start, HEAD_DIM)]

    def shuffled_blocks(columns):
        size = columns // devices
        for a in range(planes):
            for b in range(spread):
                for y in range(2):
                    yield (a * spread + b) * 2 + y, (a * 2 + y) * spread + b, size

    def copy_halves(place, weight, kept, passed):
        half = weight.shape[0] // 2
        top = place[2]
        for target, which in ((kept, top), (passed, 1 - top)):
            first = pl.multiple_of(which * half, half)
            for to, at, size in shuffled_blocks(weight.shape[1]):
                target[:, to * size : (to + 1) * size] = weight[
                    pl.ds(first, half), at * size : (at + 1) * size
                ]

    def prepare(place, images, out_grad, captions, down, *targets):
        pack_down(place, down, targets[3])
        for source, target in ((images, targets[0]), (out_grad, targets[1])):
            for to, at, size in shuffled_blocks(source.shape[1]):
                target[:, to * size : (to + 1) * size] = source[:, at * size : (at + 1) * size]
        half = captions.shape[1] // 2
        for to, at, size in shuffled_blocks(half):
            for h in range(2):
                first = 2 * at * size + h * size
                target = targets[2]
                target[:, h * half + to * size : h * half + (to + 1) * size] = captions[
                    :, first : first + size
                ]

    def natural(parts, place, source, target):
        del place
        width = source.shape[1] // parts
        for to, at, size in shuffled_blocks(width):
            for h in range(parts):
                first = parts * at * size + h * size
                target[:, first : first + size] = source[
                    :, h * width + to * size : h * width + (to + 1) * size
                ]

    def pack_self(place, query, key, value, out, own, other, kept, passed):
        copy_heads(place, (query, key, value), own, other, 0)
        copy_halves(place, out, kept, passed)

    def pack_cross(place, query, key, value, out, text, own, other, kept, passed):
        copy_heads(place, (query, key, value), own, other, 0)
        copy_halves(place, out, kept, passed)
        y, x = place[0], place[1]
        rows = query.shape[0]
        for yy, target in ((y, own), (1 - y, other)):
            start = pl.multiple_of((2 * yy + x) * TP_WIDTH, TP_WIDTH)
            size = TP_WIDTH // (2 * spread)
            for h in range(2):
                block = text[h * rows : (h + 1) * rows, pl.ds(start, TP_WIDTH)]
                for b in range(spread):
                    for yb in range(2):
                        at = (yb * spread + b) * size
                        column = (3 + h) * TP_WIDTH + (b * 2 + yb) * size
                        target[:, column : column + size] = block[:, at : at + size]

    def pack_down(place, down, payload):
        width = payload.shape[0]
        first = pl.multiple_of(place[1] * width, width)
        for to, at, size in shuffled_blocks(down.shape[1]):
            payload[:, to * size : (to + 1) * size] = down[
                pl.ds(first, width), at * size : (at + 1) * size
            ]

    def pack_up(place, up, own, other):
        y, x = place[0], place[1]
        ff_rows = up.shape[1] // devices
        width = ff_rows // 2
        for yy, target in ((y, own), (1 - y, other)):
            for a in range(planes):
                for b in range(spread):
                    start = ((a * 2 + yy) * spread + b) * ff_rows + x * width
                    column = (a * spread + b) * width
                    target[:, column : column + width] = up[
                        :, pl.ds(pl.multiple_of(start, width), width)
                    ]

    def join(place, own, other, *rest):
        payload = rest[-1]
        y = place[0]
        rows, columns = own.shape
        payload[pl.ds(pl.multiple_of(y * rows, rows), rows), :columns] = own[...]
        payload[pl.ds(pl.multiple_of((1 - y) * rows, rows), rows), :columns] = other[...]
        if len(rest) == 1:
            return
        kept, passed = rest[:2]
        half = kept.shape[0]

        def fill(source):
            for j in range(4):
                payload[j * half : (j + 1) * half, columns:] = source[
                    :, j * TP_WIDTH : (j + 1) * TP_WIDTH
                ]

        @pl.when(place[2] == place[1])
        def _():
            fill(kept)

        @pl.when(place[2] != place[1])
        def _():
            fill(passed)


    def at_place(place, write):
        for yy in range(2):
            for xx in range(2):
                pl.when((place[0] == yy) & (place[1] == xx))(lambda yy=yy, xx=xx: write(yy, xx))

    def unpack_down(place, own, other, target):
        width = own.shape[0]

        def write(y, x):
            for which, source in ((x, own), (1 - x, other)):
                for to, at, size in shuffled_blocks(own.shape[1]):
                    target[which * width : (which + 1) * width, at * size : (at + 1) * size] = (
                        source[:, to * size : (to + 1) * size].astype(F32)
                    )

        at_place(place, write)

    def unpack_up(place, *refs):
        pieces, target = refs[:4], refs[4]
        width = target.shape[1] // devices // 2

        def write(y, x):
            for k in range(4):
                yy, xx = y ^ (k // 2), x ^ (k % 2)
                for a in range(planes):
                    for b in range(spread):
                        to = ((a * 2 + yy) * spread + b) * 2 * width + xx * width
                        at = (a * spread + b) * width
                        target[:, to : to + width] = pieces[k][:, at : at + width].astype(F32)

        at_place(place, write)

    def unpack_text(place, *refs):
        pieces, target = refs[:4], refs[4]
        rows = pieces[0].shape[0]
        size = TP_WIDTH // (2 * spread)

        def write(y, x):
            for k in range(4):
                first = (2 * (y ^ (k // 2)) + (x ^ (k % 2))) * TP_WIDTH
                for h in range(2):
                    for b in range(spread):
                        for yb in range(2):
                            to = first + (yb * spread + b) * size
                            at = h * TP_WIDTH + (b * 2 + yb) * size
                            target[h * rows : (h + 1) * rows, to : to + size] = pieces[k][
                                :, at : at + size
                            ].astype(F32)

        at_place(place, write)

    def unpack_heads(place, *refs):
        pieces, halves, weights = refs[:4], refs[4:8], refs[8:11]
        out = refs[11]
        rows = out.shape[0]
        half = rows // 2

        def write(y, x):
            for k in range(4):
                yy, xx = y ^ (k // 2), x ^ (k % 2)
                for index, target in enumerate(weights):
                    for a in range(planes):
                        to = (4 * a + 2 * yy + xx) * HEAD_DIM
                        at = index * TP_WIDTH + a * HEAD_DIM
                        target[:, to : to + HEAD_DIM] = pieces[k][:, at : at + HEAD_DIM].astype(F32)
        at_place(place, write)

        def write_out(top, x):
            near = halves[:2] if top == x else halves[2:]
            for which, source in ((top, near[0]), (1 - top, near[1])):
                for to, at, size in shuffled_blocks(out.shape[1]):
                    out[which * half : (which + 1) * half, at * size : (at + 1) * size] = (
                        source[:, to * size : (to + 1) * size].astype(F32)
                    )

        for top in range(2):
            for xx in range(2):
                pl.when((place[2] == top) & (place[1] == xx))(
                    lambda top=top, xx=xx: write_out(top, xx)
                )

    def on_device(
        images,
        captions,
        cap_lengths,
        norm1_gain,
        w_query,
        w_key,
        w_value,
        w_out,
        norm2_gain,
        w_text,
        w_cross_query,
        w_cross_key,
        w_cross_value,
        w_cross_out,
        norm3_gain,
        w_up,
        w_down,
        out_grad,
    ):
        d = lax.axis_index("dp")
        x = lax.axis_index("seq")
        y = (d // spread) % 2
        top = (d % spread) // half_spread
        place = jnp.stack([y, x, top]).astype(jnp.int32)
        own_images, own_tokens, d_model = images.shape
        own_slots = captions.shape[1]
        text_d = captions.shape[2]
        ff_rows = w_down.shape[0]
        slots = 2 * own_slots
        rows = w_query.shape[0]
        half = rows // 2
        wide = 3 * TP_WIDTH
        fused = rows % 128 == 0 and half_spread == 1

        gains = gather_small(jnp.stack([norm1_gain, norm2_gain, norm3_gain]), d)
        own, other, kept, passed = whole_call(
            pack_self,
            place,
            (w_query, w_key, w_value, w_out),
            [(rows, wide), (rows, wide), (half, d_model), (half, d_model)],
        )
        other, passed = swap(other, 1, 0), flip(passed, half_spread)
        (self_load,) = whole_call(
            join, place, (own, other, kept, passed), [(2 * rows, wide + TP_WIDTH)]
        )
        self_full = gather_weight(self_load)

        cross_own, cross_other, kept, passed = whole_call(
            pack_cross,
            place,
            (after(w_cross_query, self_load, gains), w_cross_key, w_cross_value)
            + (w_cross_out, w_text),
            [(rows, 5 * TP_WIDTH), (rows, 5 * TP_WIDTH), (half, d_model), (half, d_model)],
        )
        width = ff_rows // 2
        if width % 128 == 0:
            up_own, up_other = whole_call(
                pack_up, place, (after(w_up, kept),), [(rows, width * planes * spread)] * 2
            )
        else:

            def up_columns(yy):
                return jnp.concatenate(
                    [
                        lax.dynamic_slice_in_dim(
                            w_up, ((a * 2 + yy) * spread + b) * ff_rows + x * width, width, 1
                        )
                        for a in range(planes)
                        for b in range(spread)
                    ],
                    axis=1,
                )

            up_own, up_other = up_columns(y), up_columns(1 - y)
        image_rows, out_grad_rows, caption_rows, down_load = whole_call(
            prepare,
            place,
            (
                after(images, up_own).reshape(-1, d_model),
                out_grad.reshape(-1, d_model),
                captions.reshape(-1, text_d),
                w_down,
            ),
            [(own_images * own_tokens, d_model)] * 2
            + [(own_images * own_slots, text_d), (width, d_model)],
        )
        gains = shuffle(gains.astype(F32))
        cross_other, passed = swap(cross_other, 1, 0), flip(passed, half_spread)
        up_other = swap(up_other, 1, 0)
        image_all = gather_tokens(image_rows)
        (cross_load,) = whole_call(
            join, place, (cross_own, cross_other, kept, passed), [(2 * rows, 6 * TP_WIDTH)]
        )
        cross_full = gather_weight(cross_load)
        (up_load,) = whole_call(join, place, (up_own, up_other), [(2 * rows, up_own.shape[1])])
        up_full = gather_weight(up_load)
        down_full = gather_weight(after(down_load, up_load))
        caption_all = gather_direct(after(caption_rows, image_all[1], image_all[2]))
        self_full = after(self_full, up_load)

        def head_rows(columns):
            blocks = columns.reshape(planes, 2, half_spread, 4, half, TP_WIDTH)
            blocks = blocks.transpose(0, 2, 1, 4, 3, 5)
            return blocks.reshape(TP_WIDTH, d_model)

        qkv_full, out_full = self_full[:, :wide], head_rows(self_full[:, wide:])
        cquery_full = cross_full[:, :TP_WIDTH]
        cpair_full = cross_full[:, TP_WIDTH:wide]
        text_full = jnp.concatenate(
            [cross_full[:, wide : wide + TP_WIDTH], cross_full[:, wide + TP_WIDTH : -TP_WIDTH]],
            axis=0,
        )
        cout_full = head_rows(cross_full[:, -TP_WIDTH:])

        all_lengths = jnp.concatenate([cap_lengths, swap(cap_lengths, 1, 0)])
        position = jnp.arange(own_slots)
        slot = jnp.concatenate([x * own_slots + position, (1 - x) * own_slots + position])
        usable = (slot[None, :] < all_lengths[:, None]).astype(F32)
        usable = usable.reshape(2, own_images, 1, slots)

        def by_image(pieces):
            return [piece.reshape(own_images, -1, piece.shape[-1]) for piece in pieces]

        def by_row(pieces):
            return [piece.reshape(-1, piece.shape[-1]) for piece in pieces]

        def each(multiply, pieces, weight):
            return [rounded(multiply(piece, weight)) for piece in pieces]

        def all_rows(pieces):
            return jnp.concatenate(pieces, axis=0)

        stream = image_rows.astype(F32)
        normed1 = [rounded(layer_norm(piece.astype(F32), gains[0])) for piece in image_all]
        qkv = by_image(each(mm, normed1, qkv_full))
        self_mix = by_row(per_image(self_kernel, None, qkv, [(0, TP_WIDTH)]))
        self_mix = after_all(self_mix, *caption_all)
        after_self = stream + scatter_tokens(each(mm, self_mix, out_full))[0]

        quarter = 2 * y + x

        def swap_slots(values, ky, kx):
            blocks = swap(values, ky, kx).reshape(2, 2, -1, values.shape[-1])
            blocks = blocks[::-1] if ky else blocks
            blocks = blocks[:, ::-1] if kx else blocks
            return blocks.reshape(values.shape)

        caption_rows_shape = caption_rows.shape
        caption_rows = all_rows(caption_all)
        part_feat = rounded(mm(caption_rows, text_full))
        caption_feat = jnp.zeros((part_feat.shape[0], d_model), BF16)
        for ky in range(2):
            for kx in range(2):
                piece = swap_slots(part_feat, ky, kx) if ky or kx else part_feat
                caption_feat = lax.dynamic_update_slice(
                    caption_feat, piece, (0, (quarter ^ (2 * ky + kx)) * TP_WIDTH)
                )
        cpair = rounded(mm(caption_feat, cpair_full))
        cpair = by_image(list(cpair.reshape(4, -1, 2 * TP_WIDTH)))

        normed2 = gather_tokens(rounded(layer_norm(after_self, gains[1])))
        cquery = by_image(each(mm, normed2, cquery_full))
        cross_mix = by_row(per_image(cross_kernel, usable, cquery + cpair, [(0, TP_WIDTH)]))
        after_cross = after_self + scatter_tokens(each(mm, cross_mix, cout_full))[0]

        normed3 = gather_tokens(rounded(layer_norm(after_cross, gains[2])))
        out_grad_all = gather_tokens(after(out_grad_rows, *normed3))
        active, grad_hidden, normed3, out_grad_all = feed_forward(
            normed3, out_grad_all, up_full, down_full
        )

        def pieces_of(values):
            return list(values.reshape(4, -1, values.shape[-1]))

        grad_parts = each(mm_t, pieces_of(grad_hidden), up_full)
        grad_normed3, sent3 = scatter_tokens(grad_parts)
        out_grad_all = after(out_grad_all, *grad_parts)
        grad_down_part = rounded(outer(active, out_grad_all))
        half_down = reduce_weight(grad_down_part)
        grad_up_part = rounded(outer(normed3, after(grad_hidden, grad_down_part)))
        layer_part = each(mm, pieces_of(after(active, grad_up_part, *sent3)), down_full)
        grad_normed3 = after(grad_normed3, *layer_part)
        grad_stream, grad_norm3 = norm_back(after_cross, gains[2], grad_normed3)
        grad_after_cross = out_grad_rows.astype(F32) + grad_stream

        branch2 = gather_tokens(rounded(grad_after_cross))
        up_sums = reduce_weight(after(grad_up_part, half_down, *branch2))
        down_pieces = [half_down, swap(half_down, 0, 1)]
        layer_part = after_all(layer_part, *branch2)
        layer_sum = rounded(after_cross + scatter_tokens(layer_part)[0])
        (layer_out,) = whole_call(
            functools.partial(natural, 1), place, (layer_sum,), [layer_sum.shape]
        )
        grad_cross_mix = by_image(each(mm_t, branch2, cout_full))
        back = per_image(
            cross_back_kernel,
            usable,
            cquery + cpair + grad_cross_mix,
            [(0, TP_WIDTH), (4, 2 * TP_WIDTH)],
        )
        gcquery, gcpair = by_row(back[:4]), all_rows(by_row(back[4:]))
        gcquery = after_all(gcquery, layer_sum)
        grad_parts = each(mm_t, gcquery, cquery_full)
        grad_normed2, sent2 = scatter_tokens(grad_parts)
        gcquery = list(after(tuple(gcquery), *grad_parts))
        grad_stream, grad_norm2 = norm_back(after_self, gains[1], grad_normed2)
        grad_after_self = grad_after_cross + grad_stream
        branch1 = gather_tokens(rounded(grad_after_self))

        grad_feat_part = rounded(mm_t(gcpair, cpair_full))
        grad_feat = None
        for ky in range(2):
            for kx in range(2):
                piece = lax.dynamic_slice_in_dim(
                    grad_feat_part, (quarter ^ (2 * ky + kx)) * TP_WIDTH, TP_WIDTH, 1
                )
                if ky or kx:
                    piece = after(swap_slots(piece, ky, kx), branch1[0])
                    grad_feat = grad_feat + piece.astype(F32)
                else:
                    grad_feat = piece.astype(F32)
        grad_feat = rounded(grad_feat)

        def head_blocks(parts):
            blocks = parts.reshape(planes, half_spread, 2, half, 4, TP_WIDTH)
            return blocks.transpose(0, 2, 1, 4, 3, 5).reshape(-1, TP_WIDTH)

        if fused:
            grad_cross_part = cross_weights(
                normed2, branch2, after(caption_feat, *sent2), gcquery, gcpair, cross_mix
            )
            grad_text_part = text_weights(caption_all, grad_feat)
        else:
            grad_cross_part = jnp.concatenate(
                [
                    rounded(outer(all_rows(normed2), all_rows(gcquery))),
                    rounded(outer(caption_feat, gcpair)),
                    head_blocks(rounded(outer(all_rows(cross_mix), all_rows(branch2)))),
                ],
                axis=1,
            )
            grad_text_part = rounded(outer(caption_rows, grad_feat))
            grad_text_part = jnp.concatenate(
                [grad_text_part[:d_model], grad_text_part[d_model:]], axis=1
            )
        cross_sums = reduce_weight(after(grad_cross_part, up_sums, down_pieces[1]))
        def four(summed, columns):
            own = lax.dynamic_slice(summed, (y * rows, 0), (rows, columns))
            other = lax.dynamic_slice(summed, ((1 - y) * rows, 0), (rows, columns))
            return [own, swap(own, 0, 1), swap(other, 1, 0), swap(other, 1, 1)]

        up_pieces = four(up_sums, up_sums.shape[1])
        grad_self_mix = by_image(each(mm_t, branch1, out_full))
        gqkv = by_row(per_image(self_back_kernel, None, qkv + grad_self_mix, [(0, wide)]))
        text_sums = reduce_weight(after(grad_text_part, cross_sums, *gqkv))
        grad_parts = each(mm_t, gqkv, qkv_full)
        grad_normed1, sent1 = scatter_tokens(grad_parts)
        gqkv = after_all(gqkv, *sent1)
        if fused:
            grad_self_part = self_weights(normed1, branch1, gqkv, self_mix)
        else:
            grad_self_part = jnp.concatenate(
                [
                    rounded(outer(all_rows(normed1), all_rows(gqkv))),
                    head_blocks(rounded(outer(all_rows(self_mix), all_rows(branch1)))),
                ],
                axis=1,
            )
        self_sums = reduce_weight(after(grad_self_part, text_sums, grad_normed1, *up_pieces))
        grad_stream, grad_norm1 = norm_back(stream, gains[0], grad_normed1)
        (image_grad,) = whole_call(
            functools.partial(natural, 1), place, (grad_after_self + grad_stream,), [image_rows.shape], F32
        )

        caption_part = each(mm_t, pieces_of(after(grad_feat, grad_normed1)), text_full)
        (caption_grad,) = whole_call(
            functools.partial(natural, 2), place, (scatter_tokens(caption_part)[0],), [caption_rows_shape], F32
        )
        caption_grad = caption_grad.reshape(captions.shape)


        def head_pieces(columns):
            own = columns.reshape(4, half, TP_WIDTH).transpose(1, 0, 2).reshape(half, -1)
            pairs = [
                (2 * i + j, 2 * (i ^ half_spread) + 1 - j) for i in range(devices) for j in range(2)
            ]
            far = lax.ppermute(own, ("dp", "seq"), pairs)
            return [own, flip(own, half_spread), swap(own, 0, 1), far]

        (grad_down,) = whole_call(
            unpack_down, place, down_pieces, [(2 * width, d_model)], F32
        )
        (grad_up,) = whole_call(unpack_up, place, up_pieces, [w_up.shape], F32)
        cross_pieces = four(cross_sums, wide) + head_pieces(cross_sums[:, -TP_WIDTH:])
        grad_cross_query, grad_cross_key, grad_cross_value, grad_cross_out = whole_call(
            unpack_heads, place, cross_pieces, [w_query.shape] * 4, F32
        )
        text_pieces = four(text_sums, 2 * TP_WIDTH)
        (grad_text,) = whole_call(unpack_text, place, text_pieces, [w_text.shape], F32)
        self_sums = after(self_sums, *down_pieces, *up_pieces, *cross_pieces, *text_pieces)
        self_pieces = four(self_sums, wide) + head_pieces(self_sums[:, -TP_WIDTH:])
        grad_query, grad_key, grad_value, grad_out = whole_call(
            unpack_heads, place, self_pieces, [w_query.shape] * 4, F32
        )

        norm_sums = unshuffle(jnp.stack([grad_norm1, grad_norm2, grad_norm3]))
        norm_sums = reduce_small(norm_sums, d)
        return (
            layer_out.reshape(images.shape),
            image_grad.reshape(images.shape),
            caption_grad,
            norm_sums[0],
            grad_query,
            grad_key,
            grad_value,
            grad_out,
            norm_sums[1],
            grad_text,
            grad_cross_query,
            grad_cross_key,
            grad_cross_value,
            grad_cross_out,
            norm_sums[2],
            grad_up,
            grad_down,
        )

    return on_device


def solution(mesh):
    tokens = P("dp", "seq", None)
    rows = P("dp", None)
    vector = P("dp")
    in_specs = (
        (tokens, tokens, vector)
        + (vector, rows, rows, rows, rows)
        + (vector, rows, rows, rows, rows, rows)
        + (vector, rows, rows)
        + (tokens,)
    )
    out_specs = (
        (tokens, tokens, tokens)
        + (vector, rows, rows, rows, rows)
        + (vector, rows, rows, rows, rows, rows)
        + (vector, rows, rows)
    )
    return jax.shard_map(
        make(mesh.shape["dp"]), mesh=mesh, in_specs=in_specs, out_specs=out_specs, check_vma=False
    )
```

```python
import functools

import jax
import jax.numpy as jnp
from jax import lax
from jax.experimental import pallas as pl
from jax.experimental.pallas import tpu as pltpu
from jax.sharding import PartitionSpec as P

HEADS = 16
HEAD_DIM = 128
EPSILON = 1e-05
SCALE = HEAD_DIM ** (-0.5)
BF16 = jnp.bfloat16
F32 = jnp.float32
TP_HEADS = HEADS // 4
TP_WIDTH = TP_HEADS * HEAD_DIM


def rounded(values):
    return values.astype(BF16)


def after(values, *earlier):
    return lax.optimization_barrier((values,) + earlier)[0]


def after_all(pieces, *earlier):
    return list(after(tuple(pieces), *earlier))


def mm(left, right):
    return lax.dot_general(left, right, (((1,), (0,)), ((), ())), preferred_element_type=F32)


def mm_t(left, right):
    return lax.dot_general(left, right, (((1,), (1,)), ((), ())), preferred_element_type=F32)


def outer(left, right):
    return lax.dot_general(left, right, (((0,), (0,)), ((), ())), preferred_element_type=F32)


def layer_norm(values, norm_gain):
    centred = values - jnp.mean(values, axis=-1, keepdims=True)
    spread = jnp.mean(centred * centred, axis=-1, keepdims=True)
    return centred * lax.rsqrt(spread + EPSILON) * norm_gain


def norm_back(values, norm_gain, grad_normed):
    centred = values - jnp.mean(values, axis=-1, keepdims=True)
    inverse = lax.rsqrt(jnp.mean(centred * centred, axis=-1, keepdims=True) + EPSILON)
    unit = centred * inverse
    scaled = grad_normed * norm_gain
    result = inverse * (
        scaled
        - jnp.mean(scaled, axis=-1, keepdims=True)
        - unit * jnp.mean(scaled * unit, axis=-1, keepdims=True)
    )
    return result, jnp.sum(grad_normed * unit, axis=tuple(range(values.ndim - 1)))


def join_once(pieces, target):
    rows = pieces[0].shape[0]

    @pl.when(pl.program_id(0) == 0)
    def _():
        for k in range(4):
            target[k * rows : (k + 1) * rows, :] = pieces[k][...]


def halves(rows):
    return [slice(part * rows // 2, (part + 1) * rows // 2) for part in range(2)]


def forward_kernel(*refs):
    up, active, slope, normed = refs[4:]
    join_once(refs[:4], normed)
    for here in halves(normed.shape[0]):
        hidden = mm(normed[here, :], up[...])
        half = 0.5 * (1.0 + lax.erf(hidden * (0.5**0.5)))
        active[here, :] = rounded(hidden * half)
        slope[here, :] = half + hidden * (
            jnp.exp(-0.5 * hidden * hidden) * (0.5 / jnp.pi) ** 0.5
        )


def backward_kernel(*refs):
    down, slope, grad_hidden, out_grad = refs[4:]
    join_once(refs[:4], out_grad)
    for here in halves(out_grad.shape[0]):
        grad_active = rounded(mm_t(out_grad[here, :], down[...])).astype(F32)
        grad_hidden[here, :] = rounded(slope[here, :] * grad_active)


def hidden_call(kernel, pieces, weight, weight_block, more, dtypes, block=256):
    rows, d_model = pieces[0].shape
    hidden = weight.size // d_model
    whole = pl.BlockSpec((rows, d_model), lambda i: (0, 0), pipeline_mode=pl.Buffered(1))
    column = pl.BlockSpec((4 * rows, block), lambda i: (0, i))
    return pl.pallas_call(
        kernel,
        grid=(hidden // block,),
        in_specs=[whole] * 4 + [weight_block] + [column] * len(more),
        out_specs=[column] * len(dtypes) + [pl.BlockSpec((4 * rows, d_model), lambda i: (0, 0))],
        out_shape=[jax.ShapeDtypeStruct((4 * rows, hidden), dtype) for dtype in dtypes]
        + [jax.ShapeDtypeStruct((4 * rows, d_model), BF16)],
        compiler_params=pltpu.CompilerParams(vmem_limit_bytes=56 * 1024 * 1024),
    )(*pieces, weight, *more)


def ffn_forward(normed, up, block=256):
    spec = pl.BlockSpec((up.shape[0], block), lambda i: (0, i))
    return hidden_call(forward_kernel, normed, up, spec, [], [BF16, F32], block)


def ffn_backward(out_grad, down, slope, block=256):
    spec = pl.BlockSpec((block, down.shape[1]), lambda i: (i, 0))
    return hidden_call(backward_kernel, out_grad, down, spec, [slope], [BF16], block)


def soft(queries, keys, usable):
    scores = mm_t(queries, keys) * SCALE
    if usable is not None:
        scores = jnp.where(usable, scores, -1e30)
    grown = jnp.exp(scores - jnp.max(scores, axis=-1, keepdims=True))
    return grown / jnp.sum(grown, axis=-1, keepdims=True)


def columns_at(index):
    return slice(index * HEAD_DIM, (index + 1) * HEAD_DIM)


def cut(refs, ky, index):
    return jnp.concatenate([refs[2 * ky + kx][0, :, columns_at(index)] for kx in range(2)], axis=0)


def put(refs, ky, index, values):
    rows = values.shape[0] // 2
    for kx in range(2):
        part = values[kx * rows : (kx + 1) * rows]
        refs[2 * ky + kx][0, :, columns_at(index)] = part.astype(BF16)


def attend_body(queries, pairs, key_at, value_at, usable, mix):
    for ky in range(2):
        for head in range(TP_HEADS):
            mask = None if usable is None else usable[ky, 0] > 0
            prob = soft(cut(queries, ky, head), cut(pairs, ky, key_at + head), mask)
            put(mix, ky, head, mm(rounded(prob), cut(pairs, ky, value_at + head)))


def attend_back_body(queries, pairs, key_at, value_at, usable, grads, gqueries, gpairs):
    for ky in range(2):
        for head in range(TP_HEADS):
            mask = None if usable is None else usable[ky, 0] > 0
            query_rows = cut(queries, ky, head)
            key_rows = cut(pairs, ky, key_at + head)
            grad_mix = cut(grads, ky, head)
            prob = soft(query_rows, key_rows, mask)
            grad_prob = mm_t(grad_mix, cut(pairs, ky, value_at + head))
            put(gpairs, ky, value_at + head, outer(rounded(prob), grad_mix))
            grad_scores = prob * (grad_prob - jnp.sum(prob * grad_prob, axis=-1, keepdims=True))
            grad_raw = rounded(grad_scores * SCALE)
            put(gqueries, ky, head, mm(grad_raw, key_rows))
            put(gpairs, ky, key_at + head, outer(grad_raw, query_rows))


def pieces_in(ref):
    return [ref.at[k] for k in range(4)]


def self_kernel(*refs):
    attend_body(refs[:4], refs[:4], TP_HEADS, 2 * TP_HEADS, None, pieces_in(refs[4]))


def self_back_kernel(*refs):
    target = pieces_in(refs[8])
    attend_back_body(
        refs[:4], refs[:4], TP_HEADS, 2 * TP_HEADS, None, refs[4:8], target, target
    )


def cross_kernel(usable, *refs):
    attend_body(refs[:4], refs[4:8], 0, TP_HEADS, usable, pieces_in(refs[8]))


def cross_back_kernel(usable, *refs):
    targets = [pieces_in(ref) for ref in refs[12:]]
    attend_back_body(refs[:4], refs[4:8], 0, TP_HEADS, usable, refs[8:12], *targets)


def per_image(kernel, usable, pieces, widths):
    images = pieces[0].shape[0]

    def block(shape):
        return pl.BlockSpec((1,) + tuple(shape[1:]), lambda i: (i, 0, 0))

    shapes = [(4,) + pieces[like].shape[:2] + (width,) for like, width in widths]
    in_specs = [block(piece.shape) for piece in pieces]
    if usable is not None:
        slots = usable.shape[-1]
        in_specs = [pl.BlockSpec((2, 1, 1, slots), lambda i: (0, i, 0, 0))] + in_specs
        pieces = [usable] + list(pieces)
    results = pl.pallas_call(
        kernel,
        grid=(images,),
        in_specs=in_specs,
        out_specs=[
            pl.BlockSpec((4, 1) + tuple(shape[2:]), lambda i: (0, i, 0, 0)) for shape in shapes
        ],
        out_shape=[jax.ShapeDtypeStruct(shape, BF16) for shape in shapes],
        compiler_params=pltpu.CompilerParams(vmem_limit_bytes=48 * 1024 * 1024),
    )(*pieces)
    return [result.reshape(-1, result.shape[-1]) for result in results]


def whole_call(kernel, place, args, shapes, dtype=BF16):
    vmem = pl.BlockSpec(memory_space=pltpu.VMEM)
    return pl.pallas_call(
        kernel,
        in_specs=[pl.BlockSpec(memory_space=pltpu.SMEM)] + [vmem] * len(args),
        out_specs=[vmem] * len(shapes),
        out_shape=[jax.ShapeDtypeStruct(shape, dtype) for shape in shapes],
        compiler_params=pltpu.CompilerParams(vmem_limit_bytes=48 * 1024 * 1024),
    )(place, *args)


def joined(refs):
    return jnp.concatenate([ref[...] for ref in refs], axis=0)


def put_head_rows(target, column, mix, grads):
    full = outer(mix[...], joined(grads))
    half = full.shape[0] // 2
    kept = jnp.where(pl.program_id(0) % 2 == 0, full[:half], full[half:]).astype(BF16)
    for j in range(4):
        target[j * half : (j + 1) * half, column:] = kept[:, j * TP_WIDTH : (j + 1) * TP_WIDTH]


def self_weights_kernel(*refs):
    normed, branch = refs[:4], refs[4:8]
    gqkv, mix, target = refs[8:]
    wide = 3 * TP_WIDTH
    target[:, :wide] = outer(joined(normed), gqkv[...]).astype(BF16)
    put_head_rows(target, wide, mix, branch)


def cross_weights_kernel(*refs):
    normed, branch = refs[:4], refs[4:8]
    gquery, mix, feat, gpair, target = refs[8:]
    wide = TP_WIDTH
    target[:, :wide] = outer(joined(normed), gquery[...]).astype(BF16)
    target[:, wide : 3 * wide] = outer(feat[...], gpair[...]).astype(BF16)
    put_head_rows(target, 3 * wide, mix, branch)


def text_weights_kernel(*refs):
    low, high, gfeat, target = refs[:4], refs[4:8], refs[8], refs[9]
    target[:, :TP_WIDTH] = outer(joined(low), gfeat[...]).astype(BF16)
    target[:, TP_WIDTH:] = outer(joined(high), gfeat[...]).astype(BF16)


def weight_call(kernel, d_model, columns, args, specs, blocks):
    rows = d_model // blocks
    return pl.pallas_call(
        kernel,
        grid=(blocks,),
        in_specs=specs,
        out_specs=pl.BlockSpec((rows, columns), lambda i: (i, 0)),
        out_shape=jax.ShapeDtypeStruct((d_model, columns), BF16),
        compiler_params=pltpu.CompilerParams(vmem_limit_bytes=56 * 1024 * 1024),
    )(*args)


def column_block(rows, columns, index):
    return pl.BlockSpec((rows, columns), lambda i: (0, index(i)))


def whole_block(array):
    return pl.BlockSpec(array.shape, lambda i: (0, 0), pipeline_mode=pl.Buffered(1))


def self_weights(normed, branch, gqkv, mix, blocks=8):
    tokens, d_model = normed[0].shape
    rows = d_model // blocks
    specs = [column_block(tokens, rows, lambda i: i)] * 4
    specs += [whole_block(a) for a in branch + [gqkv]]
    specs += [column_block(4 * tokens, HEAD_DIM, lambda i: i // 2)]
    args = (*normed, *branch, gqkv, mix)
    return weight_call(self_weights_kernel, d_model, 4 * TP_WIDTH, args, specs, blocks)


def cross_weights(normed, branch, feat, gquery, gpair, mix, blocks=8):
    tokens, d_model = normed[0].shape
    rows = d_model // blocks
    specs = [column_block(tokens, rows, lambda i: i)] * 4
    specs += [whole_block(a) for a in branch + [gquery]]
    specs += [column_block(4 * tokens, HEAD_DIM, lambda i: i // 2)]
    specs += [column_block(feat.shape[0], rows, lambda i: i), whole_block(gpair)]
    args = (*normed, *branch, gquery, mix, feat, gpair)
    return weight_call(cross_weights_kernel, d_model, 4 * TP_WIDTH, args, specs, blocks)


def text_weights(captions, gfeat, blocks=8):
    slots, text_d = captions[0].shape
    rows = text_d // 2 // blocks
    specs = [column_block(slots, rows, lambda i: i)] * 4
    specs += [column_block(slots, rows, lambda i: i + blocks)] * 4 + [whole_block(gfeat)]
    args = (*captions, *captions, gfeat)
    return weight_call(text_weights_kernel, text_d // 2, 2 * TP_WIDTH, args, specs, blocks)


def make(devices, planes=4):
    spread = devices // (2 * planes)
    half_spread = spread // 2
    groups = [
        [(a * 2 + y) * spread + b for a in range(planes) for b in range(spread)] for y in range(2)
    ]

    def swap(values, over_y, over_x):
        if not over_y:
            return lax.ppermute(values, "seq", [(0, 1), (1, 0)])
        if not over_x:
            return lax.ppermute(values, "dp", [(d, d ^ spread) for d in range(devices)])
        pairs = [(2 * d + x, 2 * (d ^ spread) + 1 - x) for d in range(devices) for x in range(2)]
        return lax.ppermute(values, ("dp", "seq"), pairs)

    def flip(values, bit):
        return lax.ppermute(values, "dp", [(d, d ^ bit) for d in range(devices)])

    def shuffle(values):
        lead = values.shape[:-1]
        blocks = values.reshape(lead + (planes, 2, spread, -1))
        return jnp.swapaxes(blocks, -3, -2).reshape(values.shape)

    def unshuffle(values):
        lead = values.shape[:-1]
        blocks = values.reshape(lead + (planes, spread, 2, -1))
        return jnp.swapaxes(blocks, -3, -2).reshape(values.shape)

    def gather_near(own):
        return swap(own, 0, 1), swap(own, 1, 0)

    def gather_far(own, over_x, over_y):
        half = own.shape[0] // 2
        far = jnp.concatenate([swap(over_y[:half], 0, 1), swap(over_x[half:], 1, 0)], axis=0)
        return [own, over_x, over_y, far]

    def gather_tokens(own):
        return gather_far(own, *gather_near(own))

    def gather_direct(own):
        return [own, swap(own, 0, 1), swap(own, 1, 0), swap(own, 1, 1)]

    def scatter_tokens(parts):
        here, to_x, to_y, far = lax.optimization_barrier(tuple(parts))
        half = here.shape[0] // 2
        first = (far[:half], far[half:])
        by_x, by_y = swap(first[0], 0, 1), swap(first[1], 1, 0)
        to_y = jnp.concatenate([rounded(to_y[:half].astype(F32) + by_x), to_y[half:]], axis=0)
        to_x = jnp.concatenate([to_x[:half], rounded(to_x[half:].astype(F32) + by_y)], axis=0)
        total = here.astype(F32) + swap(to_x, 0, 1).astype(F32)
        return total + swap(to_y, 1, 0).astype(F32), first, (to_x, to_y)

    def gather_weight(payload):
        return lax.all_gather(payload, "dp", axis=0, tiled=True, axis_index_groups=groups)

    def reduce_weight(parts):
        return lax.psum_scatter(
            parts, "dp", scatter_dimension=0, tiled=True, axis_index_groups=groups
        )

    def gather_small(values, d):
        bit = 1
        while bit < devices:
            other = flip(values, bit)
            low = (d & bit) == 0
            values = jnp.concatenate(
                [jnp.where(low, values, other), jnp.where(low, other, values)], axis=1
            )
            bit *= 2
        return values

    def reduce_small(values, d):
        values = values + swap(values, 0, 1)
        bit = devices // 2
        while bit:
            half = values.shape[1] // 2
            low = (d & bit) == 0
            kept = jnp.where(low, values[:, :half], values[:, half:])
            values = kept + flip(jnp.where(low, values[:, half:], values[:, :half]), bit)
            bit //= 2
        return values


    def copy_heads(place, weights, own, other, at):
        y, x = place[0], place[1]
        for yy, target in ((y, own), (1 - y, other)):
            for index, weight in enumerate(weights):
                for a in range(planes):
                    start = pl.multiple_of((4 * a + 2 * yy + x) * HEAD_DIM, HEAD_DIM)
                    column = at + index * TP_WIDTH + a * HEAD_DIM
                    target[:, column : column + HEAD_DIM] = weight[:, pl.ds(start, HEAD_DIM)]

    def shuffled_blocks(columns):
        size = columns // devices
        for a in range(planes):
            for b in range(spread):
                for y in range(2):
                    yield (a * spread + b) * 2 + y, (a * 2 + y) * spread + b, size

    def copy_halves(place, weight, kept, passed):
        half = weight.shape[0] // 2
        top = place[2]
        for target, which in ((kept, top), (passed, 1 - top)):
            first = pl.multiple_of(which * half, half)
            for to, at, size in shuffled_blocks(weight.shape[1]):
                target[:, to * size : (to + 1) * size] = weight[
                    pl.ds(first, half), at * size : (at + 1) * size
                ]

    def prepare(place, images, out_grad, captions, down, *targets):
        pack_down(place, down, targets[3])
        for source, target in ((images, targets[0]), (out_grad, targets[1])):
            for to, at, size in shuffled_blocks(source.shape[1]):
                target[:, to * size : (to + 1) * size] = source[:, at * size : (at + 1) * size]
        half = captions.shape[1] // 2
        for to, at, size in shuffled_blocks(half):
            for h in range(2):
                first = 2 * at * size + h * size
                target = targets[2]
                target[:, h * half + to * size : h * half + (to + 1) * size] = captions[
                    :, first : first + size
                ]

    def natural(parts, place, source, target):
        del place
        width = source.shape[1] // parts
        for to, at, size in shuffled_blocks(width):
            for h in range(parts):
                first = parts * at * size + h * size
                target[:, first : first + size] = source[
                    :, h * width + to * size : h * width + (to + 1) * size
                ]

    def pack_self(place, query, key, value, out, own, other, kept, passed):
        copy_heads(place, (query, key, value), own, other, 0)
        copy_halves(place, out, kept, passed)

    def pack_cross(place, query, key, value, out, text, own, other, kept, passed):
        copy_heads(place, (query, key, value), own, other, 0)
        copy_halves(place, out, kept, passed)
        y, x = place[0], place[1]
        rows = query.shape[0]
        for yy, target in ((y, own), (1 - y, other)):
            start = pl.multiple_of((2 * yy + x) * TP_WIDTH, TP_WIDTH)
            size = TP_WIDTH // (2 * spread)
            for h in range(2):
                block = text[h * rows : (h + 1) * rows, pl.ds(start, TP_WIDTH)]
                for b in range(spread):
                    for yb in range(2):
                        at = (yb * spread + b) * size
                        column = (3 + h) * TP_WIDTH + (b * 2 + yb) * size
                        target[:, column : column + size] = block[:, at : at + size]

    def pack_down(place, down, payload):
        width = payload.shape[0]
        first = pl.multiple_of(place[1] * width, width)
        for to, at, size in shuffled_blocks(down.shape[1]):
            payload[:, to * size : (to + 1) * size] = down[
                pl.ds(first, width), at * size : (at + 1) * size
            ]

    def pack_up(place, up, own, other):
        y, x = place[0], place[1]
        ff_rows = up.shape[1] // devices
        width = ff_rows // 2
        for yy, target in ((y, own), (1 - y, other)):
            for a in range(planes):
                for b in range(spread):
                    start = ((a * 2 + yy) * spread + b) * ff_rows + x * width
                    column = (a * spread + b) * width
                    target[:, column : column + width] = up[
                        :, pl.ds(pl.multiple_of(start, width), width)
                    ]

    def join(place, own, other, *rest):
        payload = rest[-1]
        y = place[0]
        rows, columns = own.shape
        payload[pl.ds(pl.multiple_of(y * rows, rows), rows), :columns] = own[...]
        payload[pl.ds(pl.multiple_of((1 - y) * rows, rows), rows), :columns] = other[...]
        if len(rest) == 1:
            return
        kept, passed = rest[:2]
        half = kept.shape[0]

        def fill(source):
            for j in range(4):
                payload[j * half : (j + 1) * half, columns:] = source[
                    :, j * TP_WIDTH : (j + 1) * TP_WIDTH
                ]

        @pl.when(place[2] == place[1])
        def _():
            fill(kept)

        @pl.when(place[2] != place[1])
        def _():
            fill(passed)


    def at_place(place, write):
        for yy in range(2):
            for xx in range(2):
                pl.when((place[0] == yy) & (place[1] == xx))(lambda yy=yy, xx=xx: write(yy, xx))

    def split(place, summed, own, other, *head):
        rows, columns = own.shape
        first = pl.multiple_of(place[0] * rows, rows)
        second = pl.multiple_of((1 - place[0]) * rows, rows)
        own[...] = summed[pl.ds(first, rows), :columns]
        other[...] = summed[pl.ds(second, rows), :columns]
        for target in head:
            half = target.shape[0]
            for j in range(4):
                target[:, j * TP_WIDTH : (j + 1) * TP_WIDTH] = summed[
                    j * half : (j + 1) * half, columns:
                ]

    def unpack_down(place, own, other, target):
        width = own.shape[0]

        def write(y, x):
            for which, source in ((x, own), (1 - x, other)):
                for to, at, size in shuffled_blocks(own.shape[1]):
                    target[which * width : (which + 1) * width, at * size : (at + 1) * size] = (
                        source[:, to * size : (to + 1) * size].astype(F32)
                    )

        at_place(place, write)

    def unpack_up(place, *refs):
        pieces, target = refs[:4], refs[4]
        width = target.shape[1] // devices // 2

        def write(y, x):
            for k in range(4):
                yy, xx = y ^ (k // 2), x ^ (k % 2)
                for a in range(planes):
                    for b in range(spread):
                        to = ((a * 2 + yy) * spread + b) * 2 * width + xx * width
                        at = (a * spread + b) * width
                        target[:, to : to + width] = pieces[k][:, at : at + width].astype(F32)

        at_place(place, write)

    def unpack_text(place, *refs):
        pieces, target = refs[:4], refs[4]
        rows = pieces[0].shape[0]
        size = TP_WIDTH // (2 * spread)

        def write(y, x):
            for k in range(4):
                first = (2 * (y ^ (k // 2)) + (x ^ (k % 2))) * TP_WIDTH
                for h in range(2):
                    for b in range(spread):
                        for yb in range(2):
                            to = first + (yb * spread + b) * size
                            at = h * TP_WIDTH + (b * 2 + yb) * size
                            target[h * rows : (h + 1) * rows, to : to + size] = pieces[k][
                                :, at : at + size
                            ].astype(F32)

        at_place(place, write)

    def unpack_heads(place, *refs):
        pieces, halves, weights = refs[:4], refs[4:8], refs[8:11]
        out = refs[11]
        rows = out.shape[0]
        half = rows // 2

        def write(y, x):
            for k in range(4):
                yy, xx = y ^ (k // 2), x ^ (k % 2)
                for index, target in enumerate(weights):
                    for a in range(planes):
                        to = (4 * a + 2 * yy + xx) * HEAD_DIM
                        at = index * TP_WIDTH + a * HEAD_DIM
                        target[:, to : to + HEAD_DIM] = pieces[k][:, at : at + HEAD_DIM].astype(F32)
        at_place(place, write)

        def write_out(top, x):
            near = halves[:2] if top == x else halves[2:]
            for which, source in ((top, near[0]), (1 - top, near[1])):
                for to, at, size in shuffled_blocks(out.shape[1]):
                    out[which * half : (which + 1) * half, at * size : (at + 1) * size] = (
                        source[:, to * size : (to + 1) * size].astype(F32)
                    )

        for top in range(2):
            for xx in range(2):
                pl.when((place[2] == top) & (place[1] == xx))(
                    lambda top=top, xx=xx: write_out(top, xx)
                )

    def on_device(
        images,
        captions,
        cap_lengths,
        norm1_gain,
        w_query,
        w_key,
        w_value,
        w_out,
        norm2_gain,
        w_text,
        w_cross_query,
        w_cross_key,
        w_cross_value,
        w_cross_out,
        norm3_gain,
        w_up,
        w_down,
        out_grad,
    ):
        d = lax.axis_index("dp")
        x = lax.axis_index("seq")
        y = (d // spread) % 2
        top = (d % spread) // half_spread
        place = jnp.stack([y, x, top]).astype(jnp.int32)
        own_images, own_tokens, d_model = images.shape
        own_slots = captions.shape[1]
        text_d = captions.shape[2]
        ff_rows = w_down.shape[0]
        slots = 2 * own_slots
        rows = w_query.shape[0]
        half = rows // 2
        wide = 3 * TP_WIDTH
        fused = rows % 128 == 0 and half_spread == 1

        own, other, kept, passed = whole_call(
            pack_self,
            place,
            (w_query, w_key, w_value, w_out),
            [(rows, wide), (rows, wide), (half, d_model), (half, d_model)],
        )
        other, passed = swap(other, 1, 0), flip(passed, half_spread)
        (self_load,) = whole_call(
            join, place, (own, other, kept, passed), [(2 * rows, wide + TP_WIDTH)]
        )
        self_full = gather_weight(self_load)

        cross_own, cross_other, kept, passed = whole_call(
            pack_cross,
            place,
            (after(w_cross_query, self_load), w_cross_key, w_cross_value)
            + (w_cross_out, w_text),
            [(rows, 5 * TP_WIDTH), (rows, 5 * TP_WIDTH), (half, d_model), (half, d_model)],
        )
        width = ff_rows // 2
        if width % 128 == 0:
            up_own, up_other = whole_call(
                pack_up, place, (after(w_up, kept),), [(rows, width * planes * spread)] * 2
            )
        else:

            def up_columns(yy):
                return jnp.concatenate(
                    [
                        lax.dynamic_slice_in_dim(
                            w_up, ((a * 2 + yy) * spread + b) * ff_rows + x * width, width, 1
                        )
                        for a in range(planes)
                        for b in range(spread)
                    ],
                    axis=1,
                )

            up_own, up_other = up_columns(y), up_columns(1 - y)
        image_rows, out_grad_rows, caption_rows, down_load = whole_call(
            prepare,
            place,
            (
                after(images, up_own).reshape(-1, d_model),
                out_grad.reshape(-1, d_model),
                captions.reshape(-1, text_d),
                w_down,
            ),
            [(own_images * own_tokens, d_model)] * 2
            + [(own_images * own_slots, text_d), (width, d_model)],
        )
        cross_other, passed = swap(cross_other, 1, 0), flip(passed, half_spread)
        up_other = swap(up_other, 1, 0)
        image_all = gather_tokens(image_rows)
        (cross_load,) = whole_call(
            join, place, (cross_own, cross_other, kept, passed), [(2 * rows, 6 * TP_WIDTH)]
        )
        cross_full = gather_weight(cross_load)
        gains = jnp.stack([norm1_gain, norm2_gain, norm3_gain])
        gains = gather_small(after(gains, image_all[1], image_all[2]), d)
        gains = shuffle(gains.astype(F32))
        up_other = after(up_other, image_all[1], image_all[2])
        (up_load,) = whole_call(join, place, (up_own, up_other), [(2 * rows, up_own.shape[1])])
        up_full = gather_weight(up_load)
        down_full = gather_weight(after(down_load, up_load))
        caption_all = gather_direct(after(caption_rows, *image_all))
        self_full = after(self_full, up_load)

        def head_rows(columns):
            blocks = columns.reshape(planes, 2, half_spread, 4, half, TP_WIDTH)
            blocks = blocks.transpose(0, 2, 1, 4, 3, 5)
            return blocks.reshape(TP_WIDTH, d_model)

        qkv_full, out_full = self_full[:, :wide], head_rows(self_full[:, wide:])
        cquery_full = cross_full[:, :TP_WIDTH]
        cpair_full = cross_full[:, TP_WIDTH:wide]
        text_full = jnp.concatenate(
            [cross_full[:, wide : wide + TP_WIDTH], cross_full[:, wide + TP_WIDTH : -TP_WIDTH]],
            axis=0,
        )
        cout_full = head_rows(cross_full[:, -TP_WIDTH:])

        all_lengths = jnp.concatenate([cap_lengths, swap(cap_lengths, 1, 0)])
        position = jnp.arange(own_slots)
        slot = jnp.concatenate([x * own_slots + position, (1 - x) * own_slots + position])
        usable = (slot[None, :] < all_lengths[:, None]).astype(F32)
        usable = usable.reshape(2, own_images, 1, slots)

        def by_image(pieces):
            return [piece.reshape(own_images, -1, piece.shape[-1]) for piece in pieces]

        def by_row(pieces):
            return [piece.reshape(-1, piece.shape[-1]) for piece in pieces]

        def all_at_once(multiply, values, weight):
            return pieces_of(rounded(multiply(values, weight)))

        def pieces_of(values):
            return list(values.reshape(4, -1, values.shape[-1]))

        def each(multiply, pieces, weight):
            return [rounded(multiply(piece, weight)) for piece in pieces]

        def all_rows(pieces):
            return jnp.concatenate(pieces, axis=0)

        stream = image_rows.astype(F32)
        normed1 = [rounded(layer_norm(piece.astype(F32), gains[0])) for piece in image_all]
        qkv = by_image(each(mm, normed1, qkv_full))
        (self_mix,) = per_image(self_kernel, None, qkv, [(0, TP_WIDTH)])
        self_mix = after(self_mix, *caption_all)
        after_self = stream + scatter_tokens(all_at_once(mm, self_mix, out_full))[0]

        quarter = 2 * y + x

        def swap_slots(values, ky, kx):
            blocks = swap(values, ky, kx).reshape(2, 2, -1, values.shape[-1])
            blocks = blocks[::-1] if ky else blocks
            blocks = blocks[:, ::-1] if kx else blocks
            return blocks.reshape(values.shape)

        caption_rows_shape = caption_rows.shape
        caption_rows = all_rows(caption_all)
        part_feat = rounded(mm(caption_rows, text_full))
        caption_feat = jnp.zeros((part_feat.shape[0], d_model), BF16)
        for ky in range(2):
            for kx in range(2):
                piece = swap_slots(part_feat, ky, kx) if ky or kx else part_feat
                caption_feat = lax.dynamic_update_slice(
                    caption_feat, piece, (0, (quarter ^ (2 * ky + kx)) * TP_WIDTH)
                )
        cpair = rounded(mm(caption_feat, cpair_full))
        cpair = by_image(list(cpair.reshape(4, -1, 2 * TP_WIDTH)))

        normed2 = gather_tokens(rounded(layer_norm(after_self, gains[1])))
        cquery = by_image(each(mm, normed2, cquery_full))
        (cross_mix,) = per_image(cross_kernel, usable, cquery + cpair, [(0, TP_WIDTH)])
        after_cross = after_self + scatter_tokens(all_at_once(mm, cross_mix, cout_full))[0]

        normed3 = gather_tokens(rounded(layer_norm(after_cross, gains[2])))
        out_grad_rows = after(out_grad_rows, *normed3)
        out_grad_near = gather_near(out_grad_rows)
        active, slope, normed3 = ffn_forward(normed3, up_full)
        out_grad_all = gather_far(out_grad_rows, *after_all(out_grad_near, active))
        grad_hidden, out_grad_all = ffn_backward(out_grad_all, down_full, slope)

        grad_parts = all_at_once(mm_t, grad_hidden, up_full)
        grad_normed3, _, sent3 = scatter_tokens(grad_parts)
        out_grad_all = after(out_grad_all, *grad_parts)
        grad_down_part = rounded(outer(active, out_grad_all))
        half_down = reduce_weight(grad_down_part)
        grad_up_part = rounded(outer(normed3, after(grad_hidden, grad_down_part)))
        layer_part = all_at_once(mm, after(active, grad_up_part, *sent3), down_full)
        grad_normed3 = after(grad_normed3, *layer_part)
        grad_stream, grad_norm3 = norm_back(after_cross, gains[2], grad_normed3)
        grad_after_cross = out_grad_rows.astype(F32) + grad_stream

        branch2 = gather_tokens(rounded(grad_after_cross))
        up_sums = reduce_weight(after(grad_up_part, half_down, *branch2))
        down_pieces = [half_down, swap(half_down, 0, 1)]
        layer_part = after_all(layer_part, *branch2)
        layer_sum = rounded(after_cross + scatter_tokens(layer_part)[0])
        (layer_out,) = whole_call(
            functools.partial(natural, 1), place, (layer_sum,), [layer_sum.shape]
        )
        grad_cross_mix = by_image(each(mm_t, branch2, cout_full))
        gcquery, gcpair = per_image(
            cross_back_kernel,
            usable,
            cquery + cpair + grad_cross_mix,
            [(0, TP_WIDTH), (4, 2 * TP_WIDTH)],
        )
        gcquery = after(gcquery, layer_sum)
        grad_parts = all_at_once(mm_t, gcquery, cquery_full)
        grad_normed2, first2, _ = scatter_tokens(grad_parts)
        gcquery = after(gcquery, *grad_parts)
        grad_stream, grad_norm2 = norm_back(after_self, gains[1], grad_normed2)
        grad_after_self = grad_after_cross + grad_stream
        branch1 = gather_tokens(rounded(grad_after_self))

        grad_feat_part = rounded(mm_t(gcpair, cpair_full))
        grad_feat = None
        for ky in range(2):
            for kx in range(2):
                piece = lax.dynamic_slice_in_dim(
                    grad_feat_part, (quarter ^ (2 * ky + kx)) * TP_WIDTH, TP_WIDTH, 1
                )
                if ky or kx:
                    piece = after(swap_slots(piece, ky, kx), branch1[0])
                    grad_feat = grad_feat + piece.astype(F32)
                else:
                    grad_feat = piece.astype(F32)
        grad_feat = rounded(grad_feat)

        def head_blocks(parts):
            blocks = parts.reshape(planes, half_spread, 2, half, 4, TP_WIDTH)
            return blocks.transpose(0, 2, 1, 4, 3, 5).reshape(-1, TP_WIDTH)

        if fused:
            grad_cross_part = cross_weights(
                normed2, branch2, after(caption_feat, *first2), gcquery, gcpair, cross_mix
            )
            grad_text_part = text_weights(caption_all, grad_feat)
        else:
            grad_cross_part = jnp.concatenate(
                [
                    rounded(outer(all_rows(normed2), gcquery)),
                    rounded(outer(caption_feat, gcpair)),
                    head_blocks(rounded(outer(cross_mix, all_rows(branch2)))),
                ],
                axis=1,
            )
            grad_text_part = rounded(outer(caption_rows, grad_feat))
            grad_text_part = jnp.concatenate(
                [grad_text_part[:d_model], grad_text_part[d_model:]], axis=1
            )
        cross_sums = reduce_weight(after(grad_cross_part, up_sums, grad_normed2))
        def four(summed):
            shape = (rows, summed.shape[1])
            own, other = whole_call(split, place, (summed,), [shape, shape])
            return [own, swap(own, 0, 1), swap(other, 1, 0), swap(other, 1, 1)]

        up_pieces = four(up_sums)
        grad_self_mix = by_image(each(mm_t, branch1, out_full))
        (gqkv,) = per_image(self_back_kernel, None, qkv + grad_self_mix, [(0, wide)])
        grad_parts = all_at_once(mm_t, after(gqkv, down_pieces[1]), qkv_full)
        text_sums = reduce_weight(after(grad_text_part, cross_sums, *grad_parts))
        grad_normed1, _, sent1 = scatter_tokens(grad_parts)
        gqkv = after(gqkv, *sent1)
        if fused:
            grad_self_part = self_weights(normed1, branch1, gqkv, self_mix)
        else:
            grad_self_part = jnp.concatenate(
                [
                    rounded(outer(all_rows(normed1), gqkv)),
                    head_blocks(rounded(outer(self_mix, all_rows(branch1)))),
                ],
                axis=1,
            )
        self_sums = reduce_weight(after(grad_self_part, text_sums, grad_normed1))
        grad_stream, grad_norm1 = norm_back(stream, gains[0], grad_normed1)
        (image_grad,) = whole_call(
            functools.partial(natural, 1), place, (grad_after_self + grad_stream,), [image_rows.shape], F32
        )

        caption_part = all_at_once(mm_t, grad_feat, text_full)
        caption_sum = scatter_tokens(after_all(caption_part, grad_normed1, *up_pieces))[0]
        (caption_grad,) = whole_call(
            functools.partial(natural, 2), place, (caption_sum,), [caption_rows_shape], F32
        )
        caption_grad = caption_grad.reshape(captions.shape)


        def seven(summed):
            shape = (rows, wide)
            own, other, head = whole_call(
                split, place, (summed,), [shape, shape, (half, d_model)]
            )
            pairs = [
                (2 * i + j, 2 * (i ^ half_spread) + 1 - j) for i in range(devices) for j in range(2)
            ]
            pieces = [own, swap(own, 0, 1), swap(other, 1, 0), swap(other, 1, 1)]
            far = lax.ppermute(head, ("dp", "seq"), pairs)
            return pieces + [head, flip(head, half_spread), swap(head, 0, 1), far]

        (grad_down,) = whole_call(
            unpack_down, place, down_pieces, [(2 * width, d_model)], F32
        )
        (grad_up,) = whole_call(unpack_up, place, up_pieces, [w_up.shape], F32)
        cross_pieces = seven(cross_sums)
        grad_cross_query, grad_cross_key, grad_cross_value, grad_cross_out = whole_call(
            unpack_heads, place, cross_pieces, [w_query.shape] * 4, F32
        )
        text_pieces = four(text_sums)
        (grad_text,) = whole_call(unpack_text, place, text_pieces, [w_text.shape], F32)
        norm_sums = jnp.stack([grad_norm1, grad_norm2, grad_norm3])
        norm_sums = unshuffle(after(norm_sums, *caption_part))
        norm_sums = reduce_small(norm_sums, d)
        self_sums = after(
            self_sums, grad_down, grad_up, grad_cross_query, grad_text, norm_sums, layer_out
        )
        self_pieces = seven(self_sums)
        grad_query, grad_key, grad_value, grad_out = whole_call(
            unpack_heads, place, self_pieces, [w_query.shape] * 4, F32
        )

        return (
            layer_out.reshape(images.shape),
            image_grad.reshape(images.shape),
            caption_grad,
            norm_sums[0],
            grad_query,
            grad_key,
            grad_value,
            grad_out,
            norm_sums[1],
            grad_text,
            grad_cross_query,
            grad_cross_key,
            grad_cross_value,
            grad_cross_out,
            norm_sums[2],
            grad_up,
            grad_down,
        )

    return on_device


def solution(mesh):
    tokens = P("dp", "seq", None)
    rows = P("dp", None)
    vector = P("dp")
    in_specs = (
        (tokens, tokens, vector)
        + (vector, rows, rows, rows, rows)
        + (vector, rows, rows, rows, rows, rows)
        + (vector, rows, rows)
        + (tokens,)
    )
    out_specs = (
        (tokens, tokens, tokens)
        + (vector, rows, rows, rows, rows)
        + (vector, rows, rows, rows, rows, rows)
        + (vector, rows, rows)
    )
    return jax.shard_map(
        make(mesh.shape["dp"]), mesh=mesh, in_specs=in_specs, out_specs=out_specs, check_vma=False
    )
```

```python
import functools

import jax
import jax.numpy as jnp
from jax import lax
from jax.experimental import pallas as pl
from jax.experimental.pallas import tpu as pltpu
from jax.sharding import PartitionSpec as P

HEADS = 16
HEAD_DIM = 128
EPSILON = 1e-05
SCALE = HEAD_DIM ** (-0.5)
BF16 = jnp.bfloat16
F32 = jnp.float32
TP_HEADS = HEADS // 4
TP_WIDTH = TP_HEADS * HEAD_DIM


def rounded(values):
    return values.astype(BF16)


def after(values, *earlier):
    return lax.optimization_barrier((values,) + earlier)[0]


def after_all(pieces, *earlier):
    return list(after(tuple(pieces), *earlier))


def mm(left, right):
    return lax.dot_general(left, right, (((1,), (0,)), ((), ())), preferred_element_type=F32)


def mm_t(left, right):
    return lax.dot_general(left, right, (((1,), (1,)), ((), ())), preferred_element_type=F32)


def outer(left, right):
    return lax.dot_general(left, right, (((0,), (0,)), ((), ())), preferred_element_type=F32)


def layer_norm(values, norm_gain):
    centred = values - jnp.mean(values, axis=-1, keepdims=True)
    spread = jnp.mean(centred * centred, axis=-1, keepdims=True)
    return centred * lax.rsqrt(spread + EPSILON) * norm_gain


def norm_back(values, norm_gain, grad_normed):
    centred = values - jnp.mean(values, axis=-1, keepdims=True)
    inverse = lax.rsqrt(jnp.mean(centred * centred, axis=-1, keepdims=True) + EPSILON)
    unit = centred * inverse
    scaled = grad_normed * norm_gain
    result = inverse * (
        scaled
        - jnp.mean(scaled, axis=-1, keepdims=True)
        - unit * jnp.mean(scaled * unit, axis=-1, keepdims=True)
    )
    return result, jnp.sum(grad_normed * unit, axis=tuple(range(values.ndim - 1)))


def join_once(pieces, target):
    rows = pieces[0].shape[0]

    @pl.when(pl.program_id(0) == 0)
    def _():
        for k in range(4):
            target[k * rows : (k + 1) * rows, :] = pieces[k][...]


def halves(rows):
    return [slice(part * rows // 2, (part + 1) * rows // 2) for part in range(2)]


def forward_kernel(*refs):
    up, active, slope, normed = refs[4:]
    join_once(refs[:4], normed)
    for here in halves(normed.shape[0]):
        hidden = mm(normed[here, :], up[...])
        half = 0.5 * (1.0 + lax.erf(hidden * (0.5**0.5)))
        active[here, :] = rounded(hidden * half)
        slope[here, :] = half + hidden * (
            jnp.exp(-0.5 * hidden * hidden) * (0.5 / jnp.pi) ** 0.5
        )


def backward_kernel(*refs):
    down, slope, grad_hidden, out_grad = refs[4:]
    join_once(refs[:4], out_grad)
    for here in halves(out_grad.shape[0]):
        grad_active = rounded(mm_t(out_grad[here, :], down[...])).astype(F32)
        grad_hidden[here, :] = rounded(slope[here, :] * grad_active)


def hidden_call(kernel, pieces, weight, weight_block, more, dtypes, block=256):
    rows, d_model = pieces[0].shape
    hidden = weight.size // d_model
    whole = pl.BlockSpec((rows, d_model), lambda i: (0, 0), pipeline_mode=pl.Buffered(1))
    column = pl.BlockSpec((4 * rows, block), lambda i: (0, i))
    return pl.pallas_call(
        kernel,
        grid=(hidden // block,),
        in_specs=[whole] * 4 + [weight_block] + [column] * len(more),
        out_specs=[column] * len(dtypes) + [pl.BlockSpec((4 * rows, d_model), lambda i: (0, 0))],
        out_shape=[jax.ShapeDtypeStruct((4 * rows, hidden), dtype) for dtype in dtypes]
        + [jax.ShapeDtypeStruct((4 * rows, d_model), BF16)],
        compiler_params=pltpu.CompilerParams(vmem_limit_bytes=56 * 1024 * 1024),
    )(*pieces, weight, *more)


def ffn_forward(normed, up, block=256):
    spec = pl.BlockSpec((up.shape[0], block), lambda i: (0, i))
    return hidden_call(forward_kernel, normed, up, spec, [], [BF16, F32], block)


def ffn_backward(out_grad, down, slope, block=256):
    spec = pl.BlockSpec((block, down.shape[1]), lambda i: (i, 0))
    return hidden_call(backward_kernel, out_grad, down, spec, [slope], [BF16], block)


def soft(queries, keys, usable):
    scores = mm_t(queries, keys) * SCALE
    if usable is not None:
        scores = jnp.where(usable, scores, -1e30)
    grown = jnp.exp(scores - jnp.max(scores, axis=-1, keepdims=True))
    return grown / jnp.sum(grown, axis=-1, keepdims=True)


def columns_at(index):
    return slice(index * HEAD_DIM, (index + 1) * HEAD_DIM)


def cut(refs, ky, index):
    return jnp.concatenate([refs[2 * ky + kx][0, :, columns_at(index)] for kx in range(2)], axis=0)


def put(refs, ky, index, values):
    rows = values.shape[0] // 2
    for kx in range(2):
        part = values[kx * rows : (kx + 1) * rows]
        refs[2 * ky + kx][0, :, columns_at(index)] = part.astype(BF16)


def attend_body(queries, pairs, key_at, value_at, usable, mix):
    for ky in range(2):
        for head in range(TP_HEADS):
            mask = None if usable is None else usable[ky, 0] > 0
            prob = soft(cut(queries, ky, head), cut(pairs, ky, key_at + head), mask)
            put(mix, ky, head, mm(rounded(prob), cut(pairs, ky, value_at + head)))


def attend_back_body(queries, pairs, key_at, value_at, usable, grads, gqueries, gpairs):
    for ky in range(2):
        for head in range(TP_HEADS):
            mask = None if usable is None else usable[ky, 0] > 0
            query_rows = cut(queries, ky, head)
            key_rows = cut(pairs, ky, key_at + head)
            grad_mix = cut(grads, ky, head)
            prob = soft(query_rows, key_rows, mask)
            grad_prob = mm_t(grad_mix, cut(pairs, ky, value_at + head))
            put(gpairs, ky, value_at + head, outer(rounded(prob), grad_mix))
            grad_scores = prob * (grad_prob - jnp.sum(prob * grad_prob, axis=-1, keepdims=True))
            grad_raw = rounded(grad_scores * SCALE)
            put(gqueries, ky, head, mm(grad_raw, key_rows))
            put(gpairs, ky, key_at + head, outer(grad_raw, query_rows))


def pieces_in(ref):
    return [ref.at[k] for k in range(4)]


def self_kernel(*refs):
    attend_body(refs[:4], refs[:4], TP_HEADS, 2 * TP_HEADS, None, pieces_in(refs[4]))


def self_back_kernel(*refs):
    target = pieces_in(refs[8])
    attend_back_body(
        refs[:4], refs[:4], TP_HEADS, 2 * TP_HEADS, None, refs[4:8], target, target
    )


def cross_kernel(usable, *refs):
    attend_body(refs[:4], refs[4:8], 0, TP_HEADS, usable, pieces_in(refs[8]))


def cross_back_kernel(usable, *refs):
    targets = [pieces_in(ref) for ref in refs[12:]]
    attend_back_body(refs[:4], refs[4:8], 0, TP_HEADS, usable, refs[8:12], *targets)


def per_image(kernel, usable, pieces, widths):
    images = pieces[0].shape[0]

    def block(shape):
        return pl.BlockSpec((1,) + tuple(shape[1:]), lambda i: (i, 0, 0))

    shapes = [(4,) + pieces[like].shape[:2] + (width,) for like, width in widths]
    in_specs = [block(piece.shape) for piece in pieces]
    if usable is not None:
        slots = usable.shape[-1]
        in_specs = [pl.BlockSpec((2, 1, 1, slots), lambda i: (0, i, 0, 0))] + in_specs
        pieces = [usable] + list(pieces)
    results = pl.pallas_call(
        kernel,
        grid=(images,),
        in_specs=in_specs,
        out_specs=[
            pl.BlockSpec((4, 1) + tuple(shape[2:]), lambda i: (0, i, 0, 0)) for shape in shapes
        ],
        out_shape=[jax.ShapeDtypeStruct(shape, BF16) for shape in shapes],
        compiler_params=pltpu.CompilerParams(vmem_limit_bytes=48 * 1024 * 1024),
    )(*pieces)
    return [result.reshape(-1, result.shape[-1]) for result in results]


def whole_call(kernel, place, args, shapes, dtype=BF16):
    vmem = pl.BlockSpec(memory_space=pltpu.VMEM)
    return pl.pallas_call(
        kernel,
        in_specs=[pl.BlockSpec(memory_space=pltpu.SMEM)] + [vmem] * len(args),
        out_specs=[vmem] * len(shapes),
        out_shape=[jax.ShapeDtypeStruct(shape, dtype) for shape in shapes],
        compiler_params=pltpu.CompilerParams(vmem_limit_bytes=48 * 1024 * 1024),
    )(place, *args)


def joined(refs):
    return jnp.concatenate([ref[...] for ref in refs], axis=0)


def put_head_rows(target, column, mix, grads):
    full = outer(mix[...], joined(grads))
    half = full.shape[0] // 2
    kept = jnp.where(pl.program_id(0) % 2 == 0, full[:half], full[half:]).astype(BF16)
    for j in range(4):
        target[j * half : (j + 1) * half, column:] = kept[:, j * TP_WIDTH : (j + 1) * TP_WIDTH]


def self_weights_kernel(*refs):
    normed, branch = refs[:4], refs[4:8]
    gqkv, mix, target = refs[8:]
    wide = 3 * TP_WIDTH
    target[:, :wide] = outer(joined(normed), gqkv[...]).astype(BF16)
    put_head_rows(target, wide, mix, branch)


def cross_weights_kernel(*refs):
    normed, branch = refs[:4], refs[4:8]
    gquery, mix, feat, gpair, target = refs[8:]
    wide = TP_WIDTH
    target[:, :wide] = outer(joined(normed), gquery[...]).astype(BF16)
    target[:, wide : 3 * wide] = outer(feat[...], gpair[...]).astype(BF16)
    put_head_rows(target, 3 * wide, mix, branch)


def text_weights_kernel(*refs):
    low, high, gfeat, target = refs[:4], refs[4:8], refs[8], refs[9]
    target[:, :TP_WIDTH] = outer(joined(low), gfeat[...]).astype(BF16)
    target[:, TP_WIDTH:] = outer(joined(high), gfeat[...]).astype(BF16)


def weight_call(kernel, d_model, columns, args, specs, blocks):
    rows = d_model // blocks
    return pl.pallas_call(
        kernel,
        grid=(blocks,),
        in_specs=specs,
        out_specs=pl.BlockSpec((rows, columns), lambda i: (i, 0)),
        out_shape=jax.ShapeDtypeStruct((d_model, columns), BF16),
        compiler_params=pltpu.CompilerParams(vmem_limit_bytes=56 * 1024 * 1024),
    )(*args)


def column_block(rows, columns, index):
    return pl.BlockSpec((rows, columns), lambda i: (0, index(i)))


def whole_block(array):
    return pl.BlockSpec(array.shape, lambda i: (0, 0), pipeline_mode=pl.Buffered(1))


def self_weights(normed, branch, gqkv, mix, blocks=8):
    tokens, d_model = normed[0].shape
    rows = d_model // blocks
    specs = [column_block(tokens, rows, lambda i: i)] * 4
    specs += [whole_block(a) for a in branch + [gqkv]]
    specs += [column_block(4 * tokens, HEAD_DIM, lambda i: i // 2)]
    args = (*normed, *branch, gqkv, mix)
    return weight_call(self_weights_kernel, d_model, 4 * TP_WIDTH, args, specs, blocks)


def cross_weights(normed, branch, feat, gquery, gpair, mix, blocks=8):
    tokens, d_model = normed[0].shape
    rows = d_model // blocks
    specs = [column_block(tokens, rows, lambda i: i)] * 4
    specs += [whole_block(a) for a in branch + [gquery]]
    specs += [column_block(4 * tokens, HEAD_DIM, lambda i: i // 2)]
    specs += [column_block(feat.shape[0], rows, lambda i: i), whole_block(gpair)]
    args = (*normed, *branch, gquery, mix, feat, gpair)
    return weight_call(cross_weights_kernel, d_model, 4 * TP_WIDTH, args, specs, blocks)


def text_weights(captions, gfeat, blocks=8):
    slots, text_d = captions[0].shape
    rows = text_d // 2 // blocks
    specs = [column_block(slots, rows, lambda i: i)] * 4
    specs += [column_block(slots, rows, lambda i: i + blocks)] * 4 + [whole_block(gfeat)]
    args = (*captions, *captions, gfeat)
    return weight_call(text_weights_kernel, text_d // 2, 2 * TP_WIDTH, args, specs, blocks)


def make(devices, planes=4):
    spread = devices // (2 * planes)
    half_spread = spread // 2
    groups = [
        [(a * 2 + y) * spread + b for a in range(planes) for b in range(spread)] for y in range(2)
    ]

    def swap(values, over_y, over_x):
        if not over_y:
            return lax.ppermute(values, "seq", [(0, 1), (1, 0)])
        if not over_x:
            return lax.ppermute(values, "dp", [(d, d ^ spread) for d in range(devices)])
        pairs = [(2 * d + x, 2 * (d ^ spread) + 1 - x) for d in range(devices) for x in range(2)]
        return lax.ppermute(values, ("dp", "seq"), pairs)

    def flip(values, bit):
        return lax.ppermute(values, "dp", [(d, d ^ bit) for d in range(devices)])

    def shuffle(values):
        lead = values.shape[:-1]
        blocks = values.reshape(lead + (planes, 2, spread, -1))
        return jnp.swapaxes(blocks, -3, -2).reshape(values.shape)

    def unshuffle(values):
        lead = values.shape[:-1]
        blocks = values.reshape(lead + (planes, spread, 2, -1))
        return jnp.swapaxes(blocks, -3, -2).reshape(values.shape)

    def gather_near(own):
        return swap(own, 0, 1), swap(own, 1, 0)

    def gather_far(own, over_x, over_y):
        half = own.shape[0] // 2
        far = jnp.concatenate([swap(over_y[:half], 0, 1), swap(over_x[half:], 1, 0)], axis=0)
        return [own, over_x, over_y, far]

    def gather_tokens(own):
        return gather_far(own, *gather_near(own))

    def gather_direct(own):
        return [own, swap(own, 0, 1), swap(own, 1, 0), swap(own, 1, 1)]

    def scatter_tokens(parts):
        here, to_x, to_y, far = lax.optimization_barrier(tuple(parts))
        half = here.shape[0] // 2
        first = (far[:half], far[half:])
        by_x, by_y = swap(first[0], 0, 1), swap(first[1], 1, 0)
        to_y = jnp.concatenate([rounded(to_y[:half].astype(F32) + by_x), to_y[half:]], axis=0)
        to_x = jnp.concatenate([to_x[:half], rounded(to_x[half:].astype(F32) + by_y)], axis=0)
        total = here.astype(F32) + swap(to_x, 0, 1).astype(F32)
        return total + swap(to_y, 1, 0).astype(F32), first, (to_x, to_y)

    def gather_weight(payload):
        return lax.all_gather(payload, "dp", axis=0, tiled=True, axis_index_groups=groups)

    def reduce_weight(parts):
        return lax.psum_scatter(
            parts, "dp", scatter_dimension=0, tiled=True, axis_index_groups=groups
        )

    def gather_small(values, d):
        bit = 1
        while bit < devices:
            other = flip(values, bit)
            low = (d & bit) == 0
            values = jnp.concatenate(
                [jnp.where(low, values, other), jnp.where(low, other, values)], axis=1
            )
            bit *= 2
        return values

    def reduce_small(values, d):
        values = values + swap(values, 0, 1)
        bit = devices // 2
        while bit:
            half = values.shape[1] // 2
            low = (d & bit) == 0
            kept = jnp.where(low, values[:, :half], values[:, half:])
            values = kept + flip(jnp.where(low, values[:, half:], values[:, :half]), bit)
            bit //= 2
        return values


    def copy_heads(place, weights, own, other, at):
        y, x = place[0], place[1]
        for yy, target in ((y, own), (1 - y, other)):
            for index, weight in enumerate(weights):
                for a in range(planes):
                    start = pl.multiple_of((4 * a + 2 * yy + x) * HEAD_DIM, HEAD_DIM)
                    column = at + index * TP_WIDTH + a * HEAD_DIM
                    target[:, column : column + HEAD_DIM] = weight[:, pl.ds(start, HEAD_DIM)]

    def shuffled_blocks(columns):
        size = columns // devices
        for a in range(planes):
            for b in range(spread):
                for y in range(2):
                    yield (a * spread + b) * 2 + y, (a * 2 + y) * spread + b, size

    def copy_halves(place, weight, kept, passed):
        half = weight.shape[0] // 2
        top = place[2]
        for target, which in ((kept, top), (passed, 1 - top)):
            first = pl.multiple_of(which * half, half)
            for to, at, size in shuffled_blocks(weight.shape[1]):
                target[:, to * size : (to + 1) * size] = weight[
                    pl.ds(first, half), at * size : (at + 1) * size
                ]

    def prepare(place, images, out_grad, captions, down, *targets):
        pack_down(place, down, targets[3])
        for source, target in ((images, targets[0]), (out_grad, targets[1])):
            for to, at, size in shuffled_blocks(source.shape[1]):
                target[:, to * size : (to + 1) * size] = source[:, at * size : (at + 1) * size]
        half = captions.shape[1] // 2
        for to, at, size in shuffled_blocks(half):
            for h in range(2):
                first = 2 * at * size + h * size
                target = targets[2]
                target[:, h * half + to * size : h * half + (to + 1) * size] = captions[
                    :, first : first + size
                ]

    def natural(parts, place, source, target):
        del place
        width = source.shape[1] // parts
        for to, at, size in shuffled_blocks(width):
            for h in range(parts):
                first = parts * at * size + h * size
                target[:, first : first + size] = source[
                    :, h * width + to * size : h * width + (to + 1) * size
                ]

    def pack_self(place, query, key, value, out, own, other, kept, passed):
        copy_heads(place, (query, key, value), own, other, 0)
        copy_halves(place, out, kept, passed)

    def pack_cross(place, query, key, value, out, text, own, other, kept, passed):
        copy_heads(place, (query, key, value), own, other, 0)
        copy_halves(place, out, kept, passed)
        y, x = place[0], place[1]
        rows = query.shape[0]
        for yy, target in ((y, own), (1 - y, other)):
            start = pl.multiple_of((2 * yy + x) * TP_WIDTH, TP_WIDTH)
            size = TP_WIDTH // (2 * spread)
            for h in range(2):
                block = text[h * rows : (h + 1) * rows, pl.ds(start, TP_WIDTH)]
                for b in range(spread):
                    for yb in range(2):
                        at = (yb * spread + b) * size
                        column = (3 + h) * TP_WIDTH + (b * 2 + yb) * size
                        target[:, column : column + size] = block[:, at : at + size]

    def pack_down(place, down, payload):
        width = payload.shape[0]
        first = pl.multiple_of(place[1] * width, width)
        for to, at, size in shuffled_blocks(down.shape[1]):
            payload[:, to * size : (to + 1) * size] = down[
                pl.ds(first, width), at * size : (at + 1) * size
            ]

    def pack_up(place, up, own, other):
        y, x = place[0], place[1]
        ff_rows = up.shape[1] // devices
        width = ff_rows // 2
        for yy, target in ((y, own), (1 - y, other)):
            for a in range(planes):
                for b in range(spread):
                    start = ((a * 2 + yy) * spread + b) * ff_rows + x * width
                    column = (a * spread + b) * width
                    target[:, column : column + width] = up[
                        :, pl.ds(pl.multiple_of(start, width), width)
                    ]

    def join(place, own, other, *rest):
        payload = rest[-1]
        y = place[0]
        rows, columns = own.shape
        payload[pl.ds(pl.multiple_of(y * rows, rows), rows), :columns] = own[...]
        payload[pl.ds(pl.multiple_of((1 - y) * rows, rows), rows), :columns] = other[...]
        if len(rest) == 1:
            return
        kept, passed = rest[:2]
        half = kept.shape[0]

        def fill(source):
            for j in range(4):
                payload[j * half : (j + 1) * half, columns:] = source[
                    :, j * TP_WIDTH : (j + 1) * TP_WIDTH
                ]

        @pl.when(place[2] == place[1])
        def _():
            fill(kept)

        @pl.when(place[2] != place[1])
        def _():
            fill(passed)


    def at_place(place, write):
        for yy in range(2):
            for xx in range(2):
                pl.when((place[0] == yy) & (place[1] == xx))(lambda yy=yy, xx=xx: write(yy, xx))

    def split(place, summed, own, other, *head):
        rows, columns = own.shape
        first = pl.multiple_of(place[0] * rows, rows)
        second = pl.multiple_of((1 - place[0]) * rows, rows)
        own[...] = summed[pl.ds(first, rows), :columns]
        other[...] = summed[pl.ds(second, rows), :columns]
        for target in head:
            half = target.shape[0]
            for j in range(4):
                target[:, j * TP_WIDTH : (j + 1) * TP_WIDTH] = summed[
                    j * half : (j + 1) * half, columns:
                ]

    def unpack_down(place, own, other, target):
        width = own.shape[0]

        def write(y, x):
            for which, source in ((x, own), (1 - x, other)):
                for to, at, size in shuffled_blocks(own.shape[1]):
                    target[which * width : (which + 1) * width, at * size : (at + 1) * size] = (
                        source[:, to * size : (to + 1) * size].astype(F32)
                    )

        at_place(place, write)

    def unpack_up(place, *refs):
        pieces, target = refs[:4], refs[4]
        width = target.shape[1] // devices // 2

        def write(y, x):
            for k in range(4):
                yy, xx = y ^ (k // 2), x ^ (k % 2)
                for a in range(planes):
                    for b in range(spread):
                        to = ((a * 2 + yy) * spread + b) * 2 * width + xx * width
                        at = (a * spread + b) * width
                        target[:, to : to + width] = pieces[k][:, at : at + width].astype(F32)

        at_place(place, write)

    def unpack_text(place, *refs):
        pieces, target = refs[:4], refs[4]
        rows = pieces[0].shape[0]
        size = TP_WIDTH // (2 * spread)

        def write(y, x):
            for k in range(4):
                first = (2 * (y ^ (k // 2)) + (x ^ (k % 2))) * TP_WIDTH
                for h in range(2):
                    for b in range(spread):
                        for yb in range(2):
                            to = first + (yb * spread + b) * size
                            at = h * TP_WIDTH + (b * 2 + yb) * size
                            target[h * rows : (h + 1) * rows, to : to + size] = pieces[k][
                                :, at : at + size
                            ].astype(F32)

        at_place(place, write)

    def unpack_heads(place, *refs):
        pieces, halves, weights = refs[:4], refs[4:8], refs[8:11]
        out = refs[11]
        rows = out.shape[0]
        half = rows // 2

        def write(y, x):
            for k in range(4):
                yy, xx = y ^ (k // 2), x ^ (k % 2)
                for index, target in enumerate(weights):
                    for a in range(planes):
                        to = (4 * a + 2 * yy + xx) * HEAD_DIM
                        at = index * TP_WIDTH + a * HEAD_DIM
                        target[:, to : to + HEAD_DIM] = pieces[k][:, at : at + HEAD_DIM].astype(F32)
        at_place(place, write)

        def write_out(top, x):
            near = halves[:2] if top == x else halves[2:]
            for which, source in ((top, near[0]), (1 - top, near[1])):
                for to, at, size in shuffled_blocks(out.shape[1]):
                    out[which * half : (which + 1) * half, at * size : (at + 1) * size] = (
                        source[:, to * size : (to + 1) * size].astype(F32)
                    )

        for top in range(2):
            for xx in range(2):
                pl.when((place[2] == top) & (place[1] == xx))(
                    lambda top=top, xx=xx: write_out(top, xx)
                )

    def on_device(
        images,
        captions,
        cap_lengths,
        norm1_gain,
        w_query,
        w_key,
        w_value,
        w_out,
        norm2_gain,
        w_text,
        w_cross_query,
        w_cross_key,
        w_cross_value,
        w_cross_out,
        norm3_gain,
        w_up,
        w_down,
        out_grad,
    ):
        d = lax.axis_index("dp")
        x = lax.axis_index("seq")
        y = (d // spread) % 2
        top = (d % spread) // half_spread
        place = jnp.stack([y, x, top]).astype(jnp.int32)
        own_images, own_tokens, d_model = images.shape
        own_slots = captions.shape[1]
        text_d = captions.shape[2]
        ff_rows = w_down.shape[0]
        slots = 2 * own_slots
        rows = w_query.shape[0]
        half = rows // 2
        wide = 3 * TP_WIDTH
        fused = rows % 128 == 0 and half_spread == 1

        own, other, kept, passed = whole_call(
            pack_self,
            place,
            (w_query, w_key, w_value, w_out),
            [(rows, wide), (rows, wide), (half, d_model), (half, d_model)],
        )
        other, passed = swap(other, 1, 0), flip(passed, half_spread)
        (self_load,) = whole_call(
            join, place, (own, other, kept, passed), [(2 * rows, wide + TP_WIDTH)]
        )
        self_full = gather_weight(self_load)

        cross_own, cross_other, kept, passed = whole_call(
            pack_cross,
            place,
            (after(w_cross_query, self_load), w_cross_key, w_cross_value)
            + (w_cross_out, w_text),
            [(rows, 5 * TP_WIDTH), (rows, 5 * TP_WIDTH), (half, d_model), (half, d_model)],
        )
        width = ff_rows // 2
        if width % 128 == 0:
            up_own, up_other = whole_call(
                pack_up, place, (after(w_up, kept),), [(rows, width * planes * spread)] * 2
            )
        else:

            def up_columns(yy):
                return jnp.concatenate(
                    [
                        lax.dynamic_slice_in_dim(
                            w_up, ((a * 2 + yy) * spread + b) * ff_rows + x * width, width, 1
                        )
                        for a in range(planes)
                        for b in range(spread)
                    ],
                    axis=1,
                )

            up_own, up_other = up_columns(y), up_columns(1 - y)
        image_rows, out_grad_rows, caption_rows, down_load = whole_call(
            prepare,
            place,
            (
                after(images, up_own).reshape(-1, d_model),
                out_grad.reshape(-1, d_model),
                captions.reshape(-1, text_d),
                w_down,
            ),
            [(own_images * own_tokens, d_model)] * 2
            + [(own_images * own_slots, text_d), (width, d_model)],
        )
        cross_other, passed = swap(cross_other, 1, 0), flip(passed, half_spread)
        up_other = swap(up_other, 1, 0)
        image_all = gather_tokens(image_rows)
        (cross_load,) = whole_call(
            join, place, (cross_own, cross_other, kept, passed), [(2 * rows, 6 * TP_WIDTH)]
        )
        cross_full = gather_weight(cross_load)
        gains = jnp.stack([norm1_gain, norm2_gain, norm3_gain])
        gains = gather_small(after(gains, image_all[1], image_all[2]), d)
        gains = shuffle(gains.astype(F32))
        up_other = after(up_other, image_all[1], image_all[2])
        (up_load,) = whole_call(join, place, (up_own, up_other), [(2 * rows, up_own.shape[1])])
        up_full = gather_weight(up_load)
        down_full = gather_weight(after(down_load, up_load))
        caption_all = gather_direct(after(caption_rows, *image_all))
        self_full = after(self_full, up_load)

        def head_rows(columns):
            blocks = columns.reshape(planes, 2, half_spread, 4, half, TP_WIDTH)
            blocks = blocks.transpose(0, 2, 1, 4, 3, 5)
            return blocks.reshape(TP_WIDTH, d_model)

        qkv_full, out_full = self_full[:, :wide], head_rows(self_full[:, wide:])
        cquery_full = cross_full[:, :TP_WIDTH]
        cpair_full = cross_full[:, TP_WIDTH:wide]
        text_full = jnp.concatenate(
            [cross_full[:, wide : wide + TP_WIDTH], cross_full[:, wide + TP_WIDTH : -TP_WIDTH]],
            axis=0,
        )
        cout_full = head_rows(cross_full[:, -TP_WIDTH:])

        all_lengths = jnp.concatenate([cap_lengths, swap(cap_lengths, 1, 0)])
        position = jnp.arange(own_slots)
        slot = jnp.concatenate([x * own_slots + position, (1 - x) * own_slots + position])
        usable = (slot[None, :] < all_lengths[:, None]).astype(F32)
        usable = usable.reshape(2, own_images, 1, slots)

        def by_image(pieces):
            return [piece.reshape(own_images, -1, piece.shape[-1]) for piece in pieces]

        def by_row(pieces):
            return [piece.reshape(-1, piece.shape[-1]) for piece in pieces]

        def all_at_once(multiply, values, weight):
            return pieces_of(rounded(multiply(values, weight)))

        def pieces_of(values):
            return list(values.reshape(4, -1, values.shape[-1]))

        def each(multiply, pieces, weight):
            return [rounded(multiply(piece, weight)) for piece in pieces]

        def all_rows(pieces):
            return jnp.concatenate(pieces, axis=0)

        stream = image_rows.astype(F32)
        normed1 = [rounded(layer_norm(piece.astype(F32), gains[0])) for piece in image_all]
        qkv = by_image(each(mm, normed1, qkv_full))
        (self_mix,) = per_image(self_kernel, None, qkv, [(0, TP_WIDTH)])
        self_mix = after(self_mix, *caption_all)
        after_self = stream + scatter_tokens(all_at_once(mm, self_mix, out_full))[0]

        quarter = 2 * y + x

        def swap_slots(values, ky, kx):
            blocks = swap(values, ky, kx).reshape(2, 2, -1, values.shape[-1])
            blocks = blocks[::-1] if ky else blocks
            blocks = blocks[:, ::-1] if kx else blocks
            return blocks.reshape(values.shape)

        caption_rows_shape = caption_rows.shape
        caption_rows = all_rows(caption_all)
        part_feat = rounded(mm(caption_rows, text_full))
        caption_feat = jnp.zeros((part_feat.shape[0], d_model), BF16)
        for ky in range(2):
            for kx in range(2):
                piece = swap_slots(part_feat, ky, kx) if ky or kx else part_feat
                caption_feat = lax.dynamic_update_slice(
                    caption_feat, piece, (0, (quarter ^ (2 * ky + kx)) * TP_WIDTH)
                )
        cpair = rounded(mm(caption_feat, cpair_full))
        cpair = by_image(list(cpair.reshape(4, -1, 2 * TP_WIDTH)))

        normed2 = gather_tokens(rounded(layer_norm(after_self, gains[1])))
        cquery = by_image(each(mm, normed2, cquery_full))
        (cross_mix,) = per_image(cross_kernel, usable, cquery + cpair, [(0, TP_WIDTH)])
        after_cross = after_self + scatter_tokens(all_at_once(mm, cross_mix, cout_full))[0]

        normed3 = gather_tokens(rounded(layer_norm(after_cross, gains[2])))
        out_grad_rows = after(out_grad_rows, *normed3)
        out_grad_near = gather_near(out_grad_rows)
        active, slope, normed3 = ffn_forward(normed3, up_full)
        out_grad_all = gather_far(out_grad_rows, *after_all(out_grad_near, active))
        grad_hidden, out_grad_all = ffn_backward(out_grad_all, down_full, slope)

        grad_parts = all_at_once(mm_t, grad_hidden, up_full)
        grad_normed3, _, sent3 = scatter_tokens(grad_parts)
        out_grad_all = after(out_grad_all, *grad_parts)
        grad_down_part = rounded(outer(active, out_grad_all))
        half_down = reduce_weight(grad_down_part)
        grad_up_part = rounded(outer(normed3, after(grad_hidden, grad_down_part)))
        layer_part = all_at_once(mm, after(active, grad_up_part, *sent3), down_full)
        grad_normed3 = after(grad_normed3, *layer_part)
        grad_stream, grad_norm3 = norm_back(after_cross, gains[2], grad_normed3)
        grad_after_cross = out_grad_rows.astype(F32) + grad_stream

        branch2 = gather_tokens(rounded(grad_after_cross))
        up_sums = reduce_weight(after(grad_up_part, half_down, *branch2))
        down_pieces = [half_down, swap(half_down, 0, 1)]
        layer_part = after_all(layer_part, *branch2)
        layer_sum = rounded(after_cross + scatter_tokens(layer_part)[0])
        (layer_out,) = whole_call(
            functools.partial(natural, 1), place, (layer_sum,), [layer_sum.shape]
        )
        grad_cross_mix = by_image(each(mm_t, branch2, cout_full))
        gcquery, gcpair = per_image(
            cross_back_kernel,
            usable,
            cquery + cpair + grad_cross_mix,
            [(0, TP_WIDTH), (4, 2 * TP_WIDTH)],
        )
        gcquery = after(gcquery, layer_sum)
        grad_parts = all_at_once(mm_t, gcquery, cquery_full)
        grad_normed2, first2, _ = scatter_tokens(grad_parts)
        gcquery = after(gcquery, *grad_parts)
        grad_stream, grad_norm2 = norm_back(after_self, gains[1], grad_normed2)
        grad_after_self = grad_after_cross + grad_stream
        branch1 = gather_tokens(rounded(grad_after_self))

        grad_feat_part = rounded(mm_t(gcpair, cpair_full))
        grad_feat = None
        for ky in range(2):
            for kx in range(2):
                piece = lax.dynamic_slice_in_dim(
                    grad_feat_part, (quarter ^ (2 * ky + kx)) * TP_WIDTH, TP_WIDTH, 1
                )
                if ky or kx:
                    piece = after(swap_slots(piece, ky, kx), branch1[0])
                    grad_feat = grad_feat + piece.astype(F32)
                else:
                    grad_feat = piece.astype(F32)
        grad_feat = rounded(grad_feat)

        def head_blocks(parts):
            blocks = parts.reshape(planes, half_spread, 2, half, 4, TP_WIDTH)
            return blocks.transpose(0, 2, 1, 4, 3, 5).reshape(-1, TP_WIDTH)

        if fused:
            grad_cross_part = cross_weights(
                normed2, branch2, after(caption_feat, *first2), gcquery, gcpair, cross_mix
            )
            grad_text_part = text_weights(caption_all, grad_feat)
        else:
            grad_cross_part = jnp.concatenate(
                [
                    rounded(outer(all_rows(normed2), gcquery)),
                    rounded(outer(caption_feat, gcpair)),
                    head_blocks(rounded(outer(cross_mix, all_rows(branch2)))),
                ],
                axis=1,
            )
            grad_text_part = rounded(outer(caption_rows, grad_feat))
            grad_text_part = jnp.concatenate(
                [grad_text_part[:d_model], grad_text_part[d_model:]], axis=1
            )
        cross_sums = reduce_weight(after(grad_cross_part, up_sums, grad_normed2))
        def four(summed):
            shape = (rows, summed.shape[1])
            own, other = whole_call(split, place, (summed,), [shape, shape])
            return [own, swap(own, 0, 1), swap(other, 1, 0), swap(other, 1, 1)]

        up_pieces = four(up_sums)
        grad_self_mix = by_image(each(mm_t, branch1, out_full))
        (gqkv,) = per_image(self_back_kernel, None, qkv + grad_self_mix, [(0, wide)])
        grad_parts = all_at_once(mm_t, after(gqkv, down_pieces[1]), qkv_full)
        text_sums = reduce_weight(after(grad_text_part, cross_sums, *grad_parts))
        grad_normed1, _, sent1 = scatter_tokens(grad_parts)
        gqkv = after(gqkv, *sent1)
        if fused:
            grad_self_part = self_weights(normed1, branch1, gqkv, self_mix)
        else:
            grad_self_part = jnp.concatenate(
                [
                    rounded(outer(all_rows(normed1), gqkv)),
                    head_blocks(rounded(outer(self_mix, all_rows(branch1)))),
                ],
                axis=1,
            )
        self_sums = reduce_weight(after(grad_self_part, text_sums, grad_normed1))
        grad_stream, grad_norm1 = norm_back(stream, gains[0], grad_normed1)
        (image_grad,) = whole_call(
            functools.partial(natural, 1), place, (grad_after_self + grad_stream,), [image_rows.shape], F32
        )

        caption_part = all_at_once(mm_t, grad_feat, text_full)
        caption_sum = scatter_tokens(after_all(caption_part, grad_normed1, *up_pieces))[0]
        (caption_grad,) = whole_call(
            functools.partial(natural, 2), place, (caption_sum,), [caption_rows_shape], F32
        )
        caption_grad = caption_grad.reshape(captions.shape)


        def seven(summed):
            shape = (rows, wide)
            own, other, head = whole_call(
                split, place, (summed,), [shape, shape, (half, d_model)]
            )
            pairs = [
                (2 * i + j, 2 * (i ^ half_spread) + 1 - j) for i in range(devices) for j in range(2)
            ]
            pieces = [own, swap(own, 0, 1), swap(other, 1, 0), swap(other, 1, 1)]
            far = lax.ppermute(head, ("dp", "seq"), pairs)
            return pieces + [head, flip(head, half_spread), swap(head, 0, 1), far]

        (grad_down,) = whole_call(
            unpack_down, place, down_pieces, [(2 * width, d_model)], F32
        )
        (grad_up,) = whole_call(unpack_up, place, up_pieces, [w_up.shape], F32)
        cross_pieces = seven(cross_sums)
        grad_cross_query, grad_cross_key, grad_cross_value, grad_cross_out = whole_call(
            unpack_heads, place, cross_pieces, [w_query.shape] * 4, F32
        )
        text_pieces = four(text_sums)
        (grad_text,) = whole_call(unpack_text, place, text_pieces, [w_text.shape], F32)
        norm_sums = jnp.stack([grad_norm1, grad_norm2, grad_norm3])
        norm_sums = unshuffle(after(norm_sums, *caption_part))
        norm_sums = reduce_small(norm_sums, d)
        self_sums = after(
            self_sums, grad_down, grad_up, norm_sums, layer_out, *cross_pieces, *text_pieces
        )
        self_pieces = seven(self_sums)
        grad_query, grad_key, grad_value, grad_out = whole_call(
            unpack_heads, place, self_pieces, [w_query.shape] * 4, F32
        )

        return (
            layer_out.reshape(images.shape),
            image_grad.reshape(images.shape),
            caption_grad,
            norm_sums[0],
            grad_query,
            grad_key,
            grad_value,
            grad_out,
            norm_sums[1],
            grad_text,
            grad_cross_query,
            grad_cross_key,
            grad_cross_value,
            grad_cross_out,
            norm_sums[2],
            grad_up,
            grad_down,
        )

    return on_device


def solution(mesh):
    tokens = P("dp", "seq", None)
    rows = P("dp", None)
    vector = P("dp")
    in_specs = (
        (tokens, tokens, vector)
        + (vector, rows, rows, rows, rows)
        + (vector, rows, rows, rows, rows, rows)
        + (vector, rows, rows)
        + (tokens,)
    )
    out_specs = (
        (tokens, tokens, tokens)
        + (vector, rows, rows, rows, rows)
        + (vector, rows, rows, rows, rows, rows)
        + (vector, rows, rows)
    )
    return jax.shard_map(
        make(mesh.shape["dp"]), mesh=mesh, in_specs=in_specs, out_specs=out_specs, check_vma=False
    )
```
